32 devices in a mesh: dp: 8 (over z, y), row: 4 (over x, core).
Axes of the slice: x: 2, y: 2, z: 4, core: 2. Of those that a mesh axis runs over, the one named last changes fastest.
Arguments:
- tokens: bfloat16 [24576, 768], P(('dp', 'row')), may hold values from -6 to 6
- ln_gain: float32 [768], replicated, may hold values from 0.5 to 1.5
- ln_bias: float32 [768], replicated, may hold values from -1.5 to 1.5
- w_query: bfloat16 [768, 768], P('dp', 'row'), may hold values from -0.21875 to 0.21875
- w_key: bfloat16 [768, 768], P('dp', 'row'), may hold values from -0.21875 to 0.21875
- w_value: bfloat16 [768, 768], P('dp', 'row'), may hold values from -0.21875 to 0.21875
- w_out: bfloat16 [768, 768], P('row', 'dp'), may hold values from -1.75 to 1.75
- w_up: bfloat16 [768, 3072], P('dp', 'row'), may hold values from -0.21875 to 0.21875
- w_down: bfloat16 [3072, 768], P('row', 'dp'), may hold values from -0.109375 to 0.109375
- doc_lengths: int32 [8, 4], P('dp'), may hold values from 1 to 1024, 3072 in all within a row
- cotangent: bfloat16 [24576, 768], P(('dp', 'row')), may hold values from -6 to 6
Outputs:
- mixed: bfloat16 [24576, 768], P(('dp', 'row'))
- input_grad: bfloat16 [24576, 768], P(('dp', 'row'))
- gain_grad: float32 [768], replicated
- bias_grad: float32 [768], replicated
- query_wgrad: float32 [768, 768], P('dp', 'row')
- key_wgrad: float32 [768, 768], P('dp', 'row')
- value_wgrad: float32 [768, 768], P('dp', 'row')
- out_wgrad: float32 [768, 768], P('row', 'dp')
- up_wgrad: float32 [768, 3072], P('dp', 'row')
- down_wgrad: float32 [3072, 768], P('row', 'dp')
The draws below stay inside these ranges and needn't reach their ends.
Inputs may be any that keep to these rules, and one draw needn't show every extreme that they name: `doc_lengths`: row k lists the lengths of the 4 documents packed in order into the 3072 tokens of index k of dp; they sum to 3072 and the longest is exactly 1024.
All inputs are finite; a program needn't handle non-finite values.
Results may differ from the reference program's by a relative error of at most 0.0099.
Values may be sent and summed in bfloat16 or wider, within the bound.
No kernel may reach another device: no remote copies, remote signals or barrier semaphores. Data moves between devices by JAX's collectives and lax.ppermute only.
A program may use at most 128 MiB of HBM per device.

```python
import math
import jax
import jax.numpy as jnp
import numpy as np
from jax import lax

D = 768
HEAD_DIM = 64
ROT_DIM = 16
FF = 3072
TOK_DEV = 3072
SEQ_MAX = 1024
DOCS = 4
QBLK = 512
TOKENS = 24576
N_DP = 8


def strengthened(drawn, own_key, source, target, blocks, factor):
    def block_of(axis_at):
        return (jnp.arange(drawn.shape[axis_at]) // (drawn.shape[axis_at] // blocks)).reshape((-1,) + (1,) * (drawn.ndim - 1 - axis_at))

    near = jax.random.permutation(own_key, blocks)[block_of(target)]
    second = (block_of(target) + blocks // 2) % blocks
    return jnp.where((block_of(source) == near) | (block_of(source) == second), factor * drawn, drawn)


def levels(stream_key, shape, split, smallest, top_value):
    def one(axis_at, blocks):
        steps = jax.random.uniform(jax.random.fold_in(jax.random.fold_in(stream_key, 6), axis_at), (blocks,), jnp.float32, smallest / len(split), top_value / len(split))
        return jnp.repeat(jnp.exp(steps), shape[axis_at] // blocks).reshape((-1,) + (1,) * (len(shape) - axis_at - 1))

    level = one(*split[0])
    for cut in split[1:]:
        level = level * one(*cut)
    return level


def profile(count, total, most, slope):
    portions = [(1 << 20) // math.isqrt(grade ** slope) + 1 for grade in range(2, count + 1)]
    spare, holding = total - most - (count - 1), [1] * (count - 1)
    while spare > 0:
        movable = [i for i in range(count - 1) if holding[i] < most]
        pool, remaining = sum([portions[i] for i in movable]), spare
        for i in movable:
            extra = min(most - holding[i], max(1, remaining * portions[i] // pool), spare)
            holding[i] = holding[i] + extra
            spare = spare - extra
    return np.array([most] + holding)


def ragged(own_key, count, total, reach, skew):
    if count == 2:
        one = jax.random.randint(own_key, (), max(1, total - reach), min(reach, total - 1) + 1)
        return jnp.stack([one, total - one])
    tallies = jnp.asarray(profile(count, total, reach, skew), jnp.int32)
    pairs = (count - 1) // 2
    giver, taker = tallies[1:1 + 2 * pairs:2], tallies[2:2 + 2 * pairs:2]
    margin = jnp.minimum(giver - 1, reach - taker)
    passed = jax.random.randint(jax.random.fold_in(own_key, 1), (pairs,), 0, 1 << 20) % (margin + 1)
    tallies = tallies.at[1:1 + 2 * pairs:2].set(giver - passed).at[2:2 + 2 * pairs:2].set(taker + passed)
    return tallies[jax.random.permutation(jax.random.fold_in(own_key, 2), count)]


def normal_values(rng, extent, width, bound, cuts=(), kind=jnp.bfloat16):
    drawn = jax.random.normal(rng, extent, jnp.float32) * width
    if len(cuts) > 0:
        drawn = levels(rng, extent, cuts, -0.22, 0.18) * drawn
    return jnp.clip(drawn, min=-bound, max=bound).astype(kind)


def bell_draw_with(own_key, extent, width, reach, split, heavy, kind=jnp.bfloat16):
    drawn = width * jax.random.normal(own_key, extent, jnp.float32)
    if split:
        drawn = drawn * levels(own_key, extent, split, -0.22, 0.18)
    return jnp.clip(strengthened(drawn, jax.random.fold_in(own_key, 3), *heavy), -reach, reach).astype(kind)


def setup_inputs(seed: int = 0) -> dict:
    key_list = jax.random.split(jax.random.key(seed), 12)
    return {
        "tokens": normal_values(key_list[0], (TOKENS, D), 1.0, 6.0, ((0, 32),)),
        "ln_gain": jnp.clip(1.0 + 0.1 * jax.random.normal(key_list[1], (D,), jnp.float32), 0.5, 1.5),
        "ln_bias": normal_values(key_list[2], (D,), 0.3, 1.5, (), jnp.float32),
        "w_query": normal_values(key_list[3], (D, D), D ** -0.5, 0.21875, ((0, 8), (1, 4))),
        "w_key": normal_values(key_list[4], (D, D), D ** -0.5, 0.21875, ((0, 8), (1, 4))),
        "w_value": normal_values(key_list[5], (D, D), D ** -0.5, 0.21875, ((0, 8), (1, 4))),
        "w_out": normal_values(key_list[6], (D, D), (D // 64) ** -0.5, 1.75, ((0, 4), (1, 8))),
        "w_up": normal_values(key_list[7], (D, FF), D ** -0.5, 0.21875, ((0, 8), (1, 4))),
        "w_down": normal_values(key_list[8], (FF, D), FF ** -0.5, 0.109375, ((0, 4), (1, 8))),
        "doc_lengths": jax.vmap(lambda own: ragged(own, DOCS, TOK_DEV, SEQ_MAX, 1))(jax.random.split(key_list[9], N_DP)).reshape((N_DP, DOCS)).astype(jnp.int32),
        "cotangent": bell_draw_with(key_list[10], (TOKENS, D), 1.0, 6.0, ((0, 32),), (0, 1, 32, 2.75)),
    }


epsilon = 1e-05
masked_value = -1000000000.0

@jax.custom_vjp
def low(v):
    return lax.optimization_barrier(v.astype(jnp.bfloat16)).astype(jnp.float32)

@jax.custom_vjp
def low_back(v):
    return v

def low_keep(v):
    return (low(v), None)

def low_pass(kept, grad):
    return (grad,)

def back_keep(v):
    return (v, None)

def back_low(kept, grad):
    return (low(grad),)
low.defvjp(low_keep, low_pass)
low_back.defvjp(back_keep, back_low)

def matmul(left, right):
    return jnp.dot(left, right, precision=lax.Precision.HIGHEST, preferred_element_type=jnp.float32)

def tables(lengths, count):
    doc_ends = jnp.cumsum(lengths).astype(jnp.int32)
    places = jnp.arange(count, dtype=jnp.int32)
    after = places[:, None] >= doc_ends[None, :]
    doc_ids = lax.optimization_barrier(jnp.sum(after.astype(jnp.int32), axis=1)).astype(jnp.int32)
    begins = lax.optimization_barrier(jnp.max(jnp.where(after, doc_ends[None, :], 0), axis=1))
    offset_f = (places - begins).astype(jnp.float32)
    half_rot = ROT_DIM // 2
    frequency = jnp.exp(-(2.0 * jnp.arange(half_rot, dtype=jnp.float32) / ROT_DIM) * math.log(10000.0))
    angle = offset_f[:, None] * frequency[None, :]
    return (doc_ids, jnp.cos(angle)[:, None, :], jnp.sin(angle)[:, None, :])

def rotate(field, cosine, sine_tab):
    half_rot = ROT_DIM // 2
    first = field[..., :half_rot]
    second = field[..., half_rot:ROT_DIM]
    return jnp.concatenate([first * cosine - second * sine_tab, second * cosine + first * sine_tab, field[..., ROT_DIM:]], axis=-1)

def layer(inputs, gain, shift, w_query, w_key, w_value, w_out, w_up, w_down, doc_ids, cosine, sine_tab):
    count = inputs.shape[0]
    heads = w_query.shape[1] // HEAD_DIM
    average = lax.optimization_barrier(jnp.mean(inputs, axis=1, keepdims=True))
    centered = inputs - average
    spread_sq = lax.optimization_barrier(jnp.mean(centered * centered, axis=1, keepdims=True))
    normed = low(centered * lax.rsqrt(spread_sq + epsilon) * gain + shift)

    def project(weight):
        return low_back(matmul(normed, weight)).reshape(count, heads, HEAD_DIM)
    queries = low(rotate(project(w_query), cosine, sine_tab))
    key_rows = low(rotate(project(w_key), cosine, sine_tab))
    value_rows = low(project(w_value))
    places = jnp.arange(count, dtype=jnp.int32)

    def attend(offset):
        query_rows = lax.dynamic_slice_in_dim(queries, offset, QBLK, 0)
        logits = jnp.einsum('qhd,khd->hqk', query_rows, key_rows, precision=lax.Precision.HIGHEST)
        scores = low_back(logits * HEAD_DIM ** (-0.5))
        own_rows = offset + jnp.arange(QBLK, dtype=jnp.int32)
        own_docs = lax.dynamic_slice_in_dim(doc_ids, offset, QBLK, 0)
        allowed = (own_docs[:, None] == doc_ids[None, :]) & (own_rows[:, None] >= places[None, :])
        scores = jnp.where(allowed[None], scores, masked_value)
        highest = lax.optimization_barrier(jnp.max(scores, axis=2, keepdims=True))
        expo = jnp.exp(scores - highest)
        attn_prob = low(expo / lax.optimization_barrier(jnp.sum(expo, axis=2, keepdims=True)))
        return jnp.einsum('hqk,khd->qhd', attn_prob, value_rows, precision=lax.Precision.HIGHEST)
    offsets = (jnp.arange(count // QBLK) * QBLK).astype(jnp.int32)
    context = lax.map(jax.checkpoint(attend), offsets).reshape(count, heads * HEAD_DIM)
    context = low_back(low(context))
    up_pre = low_back(matmul(normed, w_up))
    hidden = low(jax.nn.gelu(up_pre, approximate=False))
    return inputs + matmul(context, w_out) + matmul(hidden, w_down)

def reference(tokens, ln_gain, ln_bias, w_query, w_key, w_value, w_out, w_up, w_down, doc_lengths, cotangent):
    params = tuple((item.astype(jnp.float32) for item in (ln_gain, ln_bias, w_query, w_key, w_value, w_out, w_up, w_down)))
    shard_x = tokens.astype(jnp.float32).reshape(N_DP, TOK_DEV, D)
    shard_g = cotangent.astype(jnp.float32).reshape(N_DP, TOK_DEV, D)

    def one_shard(totals, pieces):
        inputs, seed_grad, lengths = pieces
        doc_ids, cosine, sine_tab = tables(lengths, TOK_DEV)

        def apply(inner, *weights):
            return layer(inner, *weights, doc_ids, cosine, sine_tab)
        result, puller = jax.vjp(apply, inputs, *params)
        gradients = puller(seed_grad)
        totals = tuple((a + b for a, b in zip(totals, gradients[1:])))
        return (totals, (result.astype(jnp.bfloat16), gradients[0].astype(jnp.bfloat16)))
    zeros = tuple((jnp.zeros_like(item) for item in params))
    totals, (results, input_grads) = lax.scan(one_shard, zeros, (shard_x, shard_g, doc_lengths))
    return (results.reshape(TOKENS, D), input_grads.reshape(TOKENS, D), totals[0], totals[1], totals[2], totals[3], totals[4], totals[5], totals[6], totals[7])
```

```python
from functools import partial
import math

import jax
import jax.numpy as jnp
from jax import lax
from jax.experimental import pallas as pl
from jax.experimental.pallas import tpu as pltpu
from jax.sharding import PartitionSpec as P

HEAD_DIM = 64
ROT_DIM = 16
HALF_ROT = ROT_DIM // 2
SEQ_MAX = 1024
QB = 256
EPS = 1e-05
MASKED = -1000000000.0
MIB = 1024 * 1024
F32 = jnp.float32
BF16 = jnp.bfloat16


def dot_nn(a, b):
    return lax.dot_general(a, b, (((1,), (0,)), ((), ())), preferred_element_type=F32)


def dot_nt(a, b):
    return lax.dot_general(a, b, (((1,), (1,)), ((), ())), preferred_element_type=F32)


def dot_tn(a, b):
    return lax.dot_general(a, b, (((0,), (0,)), ((), ())), preferred_element_type=F32)


def unit_of(rows):
    inputs = rows.astype(F32)
    average = jnp.mean(inputs, axis=1, keepdims=True)
    centered = inputs - average
    spread_sq = jnp.mean(centered * centered, axis=1, keepdims=True)
    inv_std = lax.rsqrt(spread_sq + EPS)
    return centered * inv_std, inv_std


def rope_t(field, cosine, sine):
    heads = field.shape[0] // HEAD_DIM
    pieces = []
    for h in range(heads):
        one = field[h * HEAD_DIM : (h + 1) * HEAD_DIM]
        first, second = one[:HALF_ROT], one[HALF_ROT:ROT_DIM]
        pieces += [
            first * cosine - second * sine,
            second * cosine + first * sine,
            one[ROT_DIM:],
        ]
    return jnp.concatenate(pieces, axis=0)


def project_kernel(me, tok, gain, bias, wat, cosine, sine, old, normed, qkv):
    unit, _ = unit_of(tok[...])
    low = (unit * gain[...] + bias[...]).astype(BF16)
    normed[...] = low
    width = qkv.shape[0] // 3
    out = dot_nt(wat[...], low)
    cos_b, sin_b = cosine[...], sine[...]
    scale = HEAD_DIM ** (-0.5)
    qkv[:width] = (rope_t(out[:width], cos_b, sin_b) * scale).astype(BF16)
    qkv[width : 2 * width] = rope_t(out[width : 2 * width], cos_b, sin_b).astype(BF16)
    qkv[2 * width :] = out[2 * width :].astype(BF16)


def project(me, rows, first, gain, bias, wat, cosine, sine, old, block=384):
    count, width = rows.shape
    total = cosine.shape[1]
    shard = total // 4
    sub = shard // block
    qkv_rows = (width // 4) * 3

    def place(b, me_ref):
        return jnp.bitwise_xor(me_ref[0], first + b // sub) * sub + b % sub

    alias = {}
    if old is None:
        old = jnp.zeros((8, 128), BF16)
    else:
        alias = {7: 1}
    return pl.pallas_call(
        project_kernel,
        grid_spec=pltpu.PrefetchScalarGridSpec(
            num_scalar_prefetch=1,
            grid=(count // block,),
            in_specs=[
                pl.BlockSpec((block, width), lambda b, m: (b, 0)),
                pl.BlockSpec((1, width), lambda b, m: (0, 0)),
                pl.BlockSpec((1, width), lambda b, m: (0, 0)),
                pl.BlockSpec((qkv_rows, width), lambda b, m: (0, 0)),
                pl.BlockSpec((HALF_ROT, block), lambda b, m: (0, place(b, m))),
                pl.BlockSpec((HALF_ROT, block), lambda b, m: (0, place(b, m))),
                pl.BlockSpec(memory_space=pl.ANY),
            ],
            out_specs=[
                pl.BlockSpec((block, width), lambda b, m: (b, 0)),
                pl.BlockSpec((qkv_rows, block), lambda b, m: (0, place(b, m))),
            ],
        ),
        out_shape=[
            jax.ShapeDtypeStruct((count, width), BF16),
            jax.ShapeDtypeStruct((qkv_rows, total), BF16),
        ],
        input_output_aliases=alias,
        compiler_params=pltpu.CompilerParams(vmem_limit_bytes=32 * MIB),
        cost_estimate=pl.CostEstimate(
            flops=2 * count * width * qkv_rows, bytes_accessed=6 * count * width, transcendentals=0
        ),
        name="project",
    )(me, rows, gain, bias, wat, cosine, sine, old)


def ffn_kernel(me, normed, grad, w_up, w_down_t, w_out, up_in, down_in, old, mlp, d_normed, d_ctx, up_g, down_g):
    @pl.when(pl.program_id(0) == 0)
    def _():
        up_g[...] = up_in[...]
        down_g[...] = down_in[...]

    n, g = normed[...], grad[...]
    up_pre = dot_nn(n, w_up[...])
    d_hidden = dot_nn(g, w_down_t[...])
    cdf = 0.5 * (1.0 + lax.erf(up_pre * (2.0**-0.5)))
    pdf = jnp.exp(-0.5 * up_pre * up_pre) * ((2.0 * math.pi) ** -0.5)
    hidden = (up_pre * cdf).astype(BF16)
    d_up = (d_hidden * (cdf + up_pre * pdf)).astype(BF16)
    d_ctx[...] = dot_nt(w_out[...], g).astype(BF16)
    mlp[...] = dot_nt(hidden, w_down_t[...]).astype(BF16)
    d_normed[...] = dot_nt(d_up, w_up[...]).astype(BF16)
    down_g[...] += dot_tn(g, hidden)
    up_g[...] += dot_tn(n, d_up)


def feed_forward(me, normed, grad, first, w_up, w_down_t, w_out, up_in, down_in, old, total, block=384):
    count, width = normed.shape
    hid = w_up.shape[1]
    shard = total // 4
    sub = shard // block
    ctx = w_out.shape[0]

    def place(b, me_ref):
        return jnp.bitwise_xor(me_ref[0], first + b // sub) * sub + b % sub

    alias = {6: 3, 7: 4}
    if old is None:
        old = jnp.zeros((8, 128), BF16)
    else:
        alias[8] = 2
    return pl.pallas_call(
        ffn_kernel,
        grid_spec=pltpu.PrefetchScalarGridSpec(
            num_scalar_prefetch=1,
            grid=(count // block,),
            in_specs=[
                pl.BlockSpec((block, width), lambda b, m: (b, 0)),
                pl.BlockSpec((block, width), lambda b, m: (b, 0)),
                pl.BlockSpec((width, hid), lambda b, m: (0, 0)),
                pl.BlockSpec((width, hid), lambda b, m: (0, 0)),
                pl.BlockSpec((ctx, width), lambda b, m: (0, 0)),
                pl.BlockSpec((width, hid), lambda b, m: (0, 0)),
                pl.BlockSpec((width, hid), lambda b, m: (0, 0)),
                pl.BlockSpec(memory_space=pl.ANY),
            ],
            out_specs=[
                pl.BlockSpec((block, width), lambda b, m: (b, 0)),
                pl.BlockSpec((block, width), lambda b, m: (b, 0)),
                pl.BlockSpec((ctx, block), lambda b, m: (0, place(b, m))),
                pl.BlockSpec((width, hid), lambda b, m: (0, 0)),
                pl.BlockSpec((width, hid), lambda b, m: (0, 0)),
            ],
        ),
        out_shape=[
            jax.ShapeDtypeStruct((count, width), BF16),
            jax.ShapeDtypeStruct((count, width), BF16),
            jax.ShapeDtypeStruct((ctx, total), BF16),
            jax.ShapeDtypeStruct((width, hid), F32),
            jax.ShapeDtypeStruct((width, hid), F32),
        ],
        input_output_aliases=alias,
        compiler_params=pltpu.CompilerParams(vmem_limit_bytes=48 * MIB),
        cost_estimate=pl.CostEstimate(
            flops=2 * count * width * (6 * hid + ctx),
            bytes_accessed=8 * count * width,
            transcendentals=2 * count * hid,
        ),
        name="feed_forward",
    )(me, normed, grad, w_up, w_down_t, w_out, up_in, down_in, old)


def attention_kernel(low_block, qkv, d_ctx, begin, cosine, sine, out, k_rows, v_rows, k_t, v_t, dk_t, dv_t):
    i = pl.program_id(0)
    width = d_ctx.shape[0]
    heads = width // HEAD_DIM
    here = pl.multiple_of(i * QB, QB)
    q_t = qkv[:width]
    k_here = qkv[width : 2 * width]
    v_here = qkv[2 * width :]
    k_t[:, pl.ds(here, QB)] = k_here
    v_t[:, pl.ds(here, QB)] = v_here
    k_nat = k_here.T
    v_nat = v_here.T
    for h in range(heads):
        cols = slice(h * HEAD_DIM, (h + 1) * HEAD_DIM)
        k_rows[h, pl.ds(here, QB), :] = k_nat[:, cols]
        v_rows[h, pl.ds(here, QB), :] = v_nat[:, cols]
    dk_t[:, pl.ds(here, QB)] = jnp.zeros((width, QB), F32)
    dv_t[:, pl.ds(here, QB)] = jnp.zeros((width, QB), F32)
    base = low_block[i]
    start = pl.multiple_of(base * QB, QB)
    reach = i - base
    first_key = begin[...] - start
    last_key = lax.broadcasted_iota(jnp.int32, (1, QB), 1) + (here - start)
    do_t = d_ctx[...]
    cos_here = cosine[:, pl.ds(here, QB)]
    sin_here = sine[:, pl.ds(here, QB)]
    scale = HEAD_DIM ** (-0.5)

    def run(blocks):
        span = blocks * QB
        key = lax.broadcasted_iota(jnp.int32, (span, QB), 0)
        allowed = (key >= first_key) & (key <= last_key)
        window = pl.ds(start, span)
        for h in range(heads):
            rows = slice(h * HEAD_DIM, (h + 1) * HEAD_DIM)
            scores = dot_nn(k_rows[h, window, :], q_t[rows])
            scores = jnp.where(allowed, scores, MASKED)
            highest = jnp.max(scores, axis=0, keepdims=True)
            expo = jnp.exp(scores - highest)
            prob = expo * (1.0 / jnp.sum(expo, axis=0, keepdims=True))
            prob_low = prob.astype(BF16)
            context = dot_nn(v_t[rows, window], prob_low)
            d_prob = dot_nn(v_rows[h, window, :], do_t[rows])
            delta = jnp.sum(do_t[rows].astype(F32) * context, axis=0, keepdims=True)
            d_scores = (prob * (d_prob - delta)).astype(BF16)
            dq = dot_nn(k_t[rows, window], d_scores) * scale
            out[rows, pl.ds(here, QB)] = rope_t(dq, cos_here, -sin_here).astype(BF16)
            out[3 * width + h * HEAD_DIM : 3 * width + (h + 1) * HEAD_DIM, pl.ds(here, QB)] = (
                context.astype(BF16)
            )
            dk_t[rows, window] += dot_nt(q_t[rows], d_scores)
            dv_t[rows, window] += dot_nt(do_t[rows], prob_low)

    for far in range(SEQ_MAX // QB + 1):
        pl.when(reach == far)(partial(run, far + 1))

    @pl.when(i == pl.num_programs(0) - 1)
    def _():
        @pl.loop(0, pl.num_programs(0))
        def _(b):
            there = pl.ds(pl.multiple_of(b * QB, QB), QB)
            out[width : 2 * width, there] = rope_t(
                dk_t[:, there], cosine[:, there], -sine[:, there]
            ).astype(BF16)
            out[2 * width : 3 * width, there] = dv_t[:, there].astype(BF16)


def attention(low_block, qkv, d_ctx, begin, cosine, sine):
    width, total = d_ctx.shape
    heads = width // HEAD_DIM
    blocks = total // QB
    return pl.pallas_call(
        attention_kernel,
        grid_spec=pltpu.PrefetchScalarGridSpec(
            num_scalar_prefetch=1,
            grid=(blocks,),
            in_specs=[
                pl.BlockSpec((3 * width, QB), lambda i, m: (0, i)),
                pl.BlockSpec((width, QB), lambda i, m: (0, i)),
                pl.BlockSpec((1, QB), lambda i, m: (0, i)),
                pl.BlockSpec((HALF_ROT, total), lambda i, m: (0, 0)),
                pl.BlockSpec((HALF_ROT, total), lambda i, m: (0, 0)),
            ],
            out_specs=pl.BlockSpec((4 * width, total), lambda i, m: (0, 0)),
            scratch_shapes=[
                pltpu.VMEM((heads, total, HEAD_DIM), BF16),
                pltpu.VMEM((heads, total, HEAD_DIM), BF16),
                pltpu.VMEM((width, total), BF16),
                pltpu.VMEM((width, total), BF16),
                pltpu.VMEM((width, total), F32),
                pltpu.VMEM((width, total), F32),
            ],
        ),
        out_shape=jax.ShapeDtypeStruct((4 * width, total), BF16),
        compiler_params=pltpu.CompilerParams(vmem_limit_bytes=48 * MIB),
        cost_estimate=pl.CostEstimate(
            flops=100 * total * SEQ_MAX * width,
            bytes_accessed=16 * total * width,
            transcendentals=heads * total * SEQ_MAX,
        ),
        name="attention",
    )(low_block, qkv, d_ctx, begin, cosine, sine)


def finish_kernel(me, heads_t, tok, normed, grad, mlp, d_mlp, wat, weight_in, sums_in, summed, d_normed, weight_g, sums):
    @pl.when(pl.program_id(0) == 0)
    def _():
        weight_g[...] = weight_in[...]
        sums[...] = sums_in[...]

    cut = (heads_t.shape[0] // 4) * 3
    both = heads_t[...]
    rows = both.T
    summed[...] = (dot_nn(rows[:, cut:], wat[cut:]) + mlp[...].astype(F32)).astype(BF16)
    total = dot_nn(rows[:, :cut], wat[:cut]) + d_mlp[...].astype(F32)
    d_normed[...] = total.astype(BF16)
    weight_g[:cut] += dot_nn(both[:cut], normed[...])
    weight_g[cut:] += dot_nn(both[cut:], grad[...])
    unit, _ = unit_of(tok[...])
    sums[0:1] += jnp.sum(total * unit, axis=0, keepdims=True)
    sums[1:2] += jnp.sum(total, axis=0, keepdims=True)


def finish(me, heads_t, tok, normed, grad, mlp, d_mlp, wat, weight_in, sums_in, first, block=384):
    count, width = normed.shape
    total = heads_t.shape[1]
    shard = total // 4
    sub = shard // block

    def place(b, me_ref):
        return jnp.bitwise_xor(me_ref[0], first + b // sub) * sub + b % sub

    row_spec = pl.BlockSpec((block, width), lambda b, m: (b, 0))
    square = pl.BlockSpec((width, width), lambda b, m: (0, 0))
    sums_spec = pl.BlockSpec((8, width), lambda b, m: (0, 0))
    return pl.pallas_call(
        finish_kernel,
        grid_spec=pltpu.PrefetchScalarGridSpec(
            num_scalar_prefetch=1,
            grid=(count // block,),
            in_specs=[
                pl.BlockSpec((width, block), lambda b, m: (0, place(b, m))),
                row_spec,
                row_spec,
                row_spec,
                row_spec,
                row_spec,
                square,
                square,
                sums_spec,
            ],
            out_specs=[row_spec, row_spec, square, sums_spec],
        ),
        out_shape=[
            jax.ShapeDtypeStruct((count, width), BF16),
            jax.ShapeDtypeStruct((count, width), BF16),
            jax.ShapeDtypeStruct((width, width), F32),
            jax.ShapeDtypeStruct((8, width), F32),
        ],
        input_output_aliases={8: 2, 9: 3},
        compiler_params=pltpu.CompilerParams(vmem_limit_bytes=48 * MIB),
        cost_estimate=pl.CostEstimate(
            flops=4 * count * width * width, bytes_accessed=14 * count * width, transcendentals=0
        ),
        name="finish",
    )(me, heads_t, tok, normed, grad, mlp, d_mlp, wat, weight_in, sums_in)


def swap(value, axis, size, bit):
    return lax.ppermute(value, axis, [(i, i ^ bit) for i in range(size)])


def bits_of(size):
    out, bit = [], 1
    while bit < size:
        out.append(bit)
        bit *= 2
    return out


def gather_rows(shard, size, me):
    held = shard[None]
    for bit in reversed(bits_of(size)):
        theirs = swap(held, "dp", size, bit)
        mine_second = (me & bit) != 0
        low = jnp.where(mine_second, theirs, held)
        high = jnp.where(mine_second, held, theirs)
        held = jnp.stack([low, high], axis=1).reshape((-1,) + shard.shape)
    return held.reshape(size * shard.shape[0], shard.shape[1])


def scatter_rows(whole, size, me):
    rows, width = whole.shape
    held = whole.reshape(size, rows // size, width)
    for bit in bits_of(size):
        pairs = held.reshape(held.shape[0] // 2, 2, rows // size, width)
        mine = ((me & bit) != 0).astype(jnp.int32)
        keep = lax.dynamic_index_in_dim(pairs, mine, 1, keepdims=False)
        send = lax.dynamic_index_in_dim(pairs, 1 - mine, 1, keepdims=False)
        theirs = swap(send.astype(BF16), "dp", size, bit)
        held = keep + theirs.astype(F32)
    return held[0]


def sum_over(value, axes):
    for axis, size in axes:
        for bit in bits_of(size):
            value = value + swap(value, axis, size, bit)
    return value


def tables(lengths, count):
    doc_ends = jnp.cumsum(lengths)
    places = jnp.arange(count, dtype=jnp.int32)
    after = places[:, None] >= doc_ends[None, :]
    begins = jnp.max(jnp.where(after, doc_ends[None, :], 0), axis=1)
    offset_f = (places - begins).astype(F32)
    frequency = jnp.exp(
        -(2.0 * jnp.arange(HALF_ROT, dtype=F32) / ROT_DIM) * math.log(10000.0)
    )
    angle = frequency[:, None] * offset_f[None, :]
    low_block = begins.reshape(count // QB, QB)[:, 0] // QB
    return begins[None, :], low_block, jnp.cos(angle), jnp.sin(angle)


def body(
    n_dp, n_row, tokens, ln_gain, ln_bias, w_query, w_key, w_value, w_out, w_up, w_down, doc_lengths, cotangent
):
    shard, width = tokens.shape
    total = shard * n_row
    dp_me = lax.axis_index("dp")
    row_me = lax.axis_index("row")
    me = row_me.astype(jnp.int32).reshape(1)
    core, chip = 1, 2

    attn_w = gather_rows(jnp.concatenate([w_query, w_key, w_value, w_out.T], axis=1), n_dp, dp_me)
    up_w = gather_rows(w_up, n_dp, dp_me)
    down_w = gather_rows(w_down.T, n_dp, dp_me)
    wat = attn_w.T
    cut = (width // 4) * 3

    tok_core = swap(tokens, "row", n_row, core)
    tok_chip = swap(tokens, "row", n_row, chip)
    near_tok = jnp.concatenate([tokens, tok_core], axis=0)
    far_tok = jnp.concatenate([tok_chip, swap(tok_chip, "row", n_row, core)], axis=0)
    later, tok_chip = lax.optimization_barrier((cotangent, tok_chip))
    g_core = swap(cotangent, "row", n_row, core)
    g_chip = swap(later, "row", n_row, chip)
    near_g = jnp.concatenate([cotangent, g_core], axis=0)
    far_g = jnp.concatenate([g_chip, swap(g_chip, "row", n_row, core)], axis=0)

    begin, low_block, cosine, sine = tables(doc_lengths[0], total)
    gain, bias = ln_gain[None, :], ln_bias[None, :]

    near_n, qkv = project(me, near_tok, 0, gain, bias, wat, cosine, sine, None)
    zero = jnp.zeros((width, up_w.shape[1]), F32)
    near_mlp, near_dm, d_ctx, up_g, down_g = feed_forward(
        me, near_n, near_g, 0, up_w, down_w, wat[cut:], zero, zero, None, total
    )
    far_n, qkv = project(me, far_tok, 2, gain, bias, wat, cosine, sine, qkv)
    far_mlp, far_dm, d_ctx, up_g, down_g = feed_forward(
        me, far_n, far_g, 2, up_w, down_w, wat[cut:], up_g, down_g, d_ctx, total
    )
    up_wgrad = scatter_rows(up_g, n_dp, dp_me)
    down_wgrad = scatter_rows(down_g, n_dp, dp_me).T

    heads_t = attention(low_block, qkv, d_ctx, begin, cosine, sine)

    zero_w = jnp.zeros((width, width), F32)
    far_sum, far_dn, attn_g, sums = finish(
        me, heads_t, far_tok, far_n, far_g, far_mlp, far_dm, wat, zero_w, jnp.zeros((8, width), F32), 2
    )

    def across(far):
        theirs = swap(far[shard:], "row", n_row, core)
        both = (far[:shard].astype(F32) + theirs.astype(F32)).astype(BF16)
        return swap(both, "row", n_row, chip)

    dn_chip = across(far_dn)
    sum_chip = across(far_sum)
    near_sum, near_dn, attn_g, sums = finish(
        me, heads_t, near_tok, near_n, near_g, near_mlp, near_dm, wat, attn_g, sums, 0
    )
    dn_core = swap(near_dn[shard:], "row", n_row, core)
    sum_core = swap(near_sum[shard:], "row", n_row, core)
    sums = sum_over(sums, (("row", n_row), ("dp", n_dp)))
    attn_wgrad = scatter_rows(attn_g.T, n_dp, dp_me)

    summed = near_sum[:shard].astype(F32) + sum_core.astype(F32) + sum_chip.astype(F32)
    mixed = (tokens.astype(F32) + summed).astype(BF16)
    norm_share = near_dn[:shard].astype(F32) + dn_core.astype(F32) + dn_chip.astype(F32)
    unit, inv_std = unit_of(tokens)
    unit_grad = norm_share * ln_gain
    plain_mean = jnp.sum(unit_grad, axis=1, keepdims=True) / width
    cross_mean = jnp.sum(unit_grad * unit, axis=1, keepdims=True) / width
    input_grad = (
        cotangent.astype(F32) + inv_std * (unit_grad - plain_mean - unit * cross_mean)
    ).astype(BF16)

    third = width // 4
    return (
        mixed,
        input_grad,
        sums[0],
        sums[1],
        attn_wgrad[:, :third],
        attn_wgrad[:, third : 2 * third],
        attn_wgrad[:, 2 * third : 3 * third],
        attn_wgrad[:, 3 * third :].T,
        up_wgrad,
        down_wgrad,
    )


def solution(mesh):
    in_specs = (
        P(("dp", "row"), None),
        P(),
        P(),
        P("dp", "row"),
        P("dp", "row"),
        P("dp", "row"),
        P("row", "dp"),
        P("dp", "row"),
        P("row", "dp"),
        P("dp", None),
        P(("dp", "row"), None),
    )
    out_specs = (
        P(("dp", "row"), None),
        P(("dp", "row"), None),
        P(),
        P(),
        P("dp", "row"),
        P("dp", "row"),
        P("dp", "row"),
        P("row", "dp"),
        P("dp", "row"),
        P("row", "dp"),
    )
    sizes = (mesh.shape["dp"], mesh.shape["row"])
    return jax.shard_map(
        partial(body, *sizes), mesh=mesh, in_specs=in_specs, out_specs=out_specs, check_vma=False
    )
```

```python
from functools import partial
import math

import jax
import jax.numpy as jnp
from jax import lax
from jax.experimental import pallas as pl
from jax.experimental.pallas import tpu as pltpu
from jax.sharding import PartitionSpec as P

HEAD_DIM = 64
ROT_DIM = 16
HALF_ROT = ROT_DIM // 2
SEQ_MAX = 1024
QB = 256
EPS = 1e-05
MASKED = -1000000000.0
MIB = 1024 * 1024
F32 = jnp.float32
BF16 = jnp.bfloat16


def dot_nn(a, b):
    return lax.dot_general(a, b, (((1,), (0,)), ((), ())), preferred_element_type=F32)


def dot_nt(a, b):
    return lax.dot_general(a, b, (((1,), (1,)), ((), ())), preferred_element_type=F32)


def dot_tn(a, b):
    return lax.dot_general(a, b, (((0,), (0,)), ((), ())), preferred_element_type=F32)


def unit_of(rows):
    inputs = rows.astype(F32)
    average = jnp.mean(inputs, axis=1, keepdims=True)
    centered = inputs - average
    spread_sq = jnp.mean(centered * centered, axis=1, keepdims=True)
    inv_std = lax.rsqrt(spread_sq + EPS)
    return centered * inv_std, inv_std


def rope_t(field, cosine, sine):
    heads = field.shape[0] // HEAD_DIM
    pieces = []
    for h in range(heads):
        one = field[h * HEAD_DIM : (h + 1) * HEAD_DIM]
        first, second = one[:HALF_ROT], one[HALF_ROT:ROT_DIM]
        pieces += [
            first * cosine - second * sine,
            second * cosine + first * sine,
            one[ROT_DIM:],
        ]
    return jnp.concatenate(pieces, axis=0)


def params(limit=56):
    return pltpu.CompilerParams(vmem_limit_bytes=limit * MIB)


def placing(first, sub):
    def place(b, me_ref):
        return jnp.bitwise_xor(me_ref[0], first + b // sub) * sub + b % sub

    return place


def list_specs(block, width, sub, count):
    return [
        pl.BlockSpec((block, width), lambda b, m, k=k: (jnp.clip(b - k * sub, 0, sub - 1), 0))
        for k in range(count)
    ]


def waiting(kernel, scalars, operands, deps):
    ahead = scalars + operands

    def run(*refs):
        kernel(*refs[:ahead], *refs[ahead + deps :])

    return run


def of_list(refs):
    part = pl.num_programs(0) // len(refs)
    out = refs[0][...]
    for k in range(1, len(refs)):
        out = jnp.where(pl.program_id(0) >= k * part, refs[k][...], out)
    return out


def put_list(refs, value):
    part = pl.num_programs(0) // len(refs)
    for k, ref in enumerate(refs):

        @pl.when(pl.program_id(0) // part == k)
        def _():
            ref[...] = value


def cost(micros):
    return pl.CostEstimate(flops=int(micros * 9.612e+07), bytes_accessed=1, transcendentals=0)


def ffn_kernel(tok_a, tok_b, g_a, g_b, gain, bias, w_up, w_down_t, *rest):
    hid = w_up.shape[1]
    last = len(rest) > 5
    if last:
        sofar, normed, mlp_a, mlp_b, d_normed, weight_out, weight_g = rest
    else:
        normed, mlp_a, mlp_b, d_normed, weight_g = rest

    @pl.when(pl.program_id(0) == 0)
    def _():
        weight_g[...] = sofar[...] if last else jnp.zeros_like(weight_g)

    unit, _ = unit_of(of_list([tok_a, tok_b]))
    n, g = (unit * gain[...] + bias[...]).astype(BF16), of_list([g_a, g_b])
    normed[...] = n
    up_pre = dot_nn(n, w_up[...])
    d_hidden = dot_nn(g, w_down_t[...])
    cdf = 0.5 * (1.0 + lax.erf(up_pre * (2.0**-0.5)))
    pdf = jnp.exp(-0.5 * up_pre * up_pre) * ((2.0 * math.pi) ** -0.5)
    hidden = (up_pre * cdf).astype(BF16)
    d_up = (d_hidden * (cdf + up_pre * pdf)).astype(BF16)
    put_list([mlp_a, mlp_b], dot_nt(hidden, w_down_t[...]).astype(BF16))
    d_normed[...] = dot_nt(d_up, w_up[...]).astype(BF16)
    weight_g[:, :hid] += dot_tn(n, d_up)
    weight_g[:, hid:] += dot_tn(g, hidden)
    if last:

        @pl.when(pl.program_id(0) == pl.num_programs(0) - 1)
        def _():
            weight_out[...] = weight_g[...].astype(BF16)


def feed_forward(toks, grads, gain, bias, w_up, w_down_t, sofar, deps=(), block=384):
    shard, width = grads[0].shape
    count = 2 * shard
    hid = w_up.shape[1]
    sub = shard // block
    row = pl.BlockSpec((block, width), lambda b: (b, 0))
    half = [
        pl.BlockSpec((block, width), lambda b, k=k: (jnp.clip(b - k * sub, 0, sub - 1), 0))
        for k in range(2)
    ]
    one = pl.BlockSpec((1, width), lambda b: (0, 0))
    square = pl.BlockSpec((width, hid), lambda b: (0, 0))
    double = pl.BlockSpec((width, 2 * hid), lambda b: (0, 0))
    return pl.pallas_call(
        waiting(ffn_kernel, 0, 8 + len(sofar), len(deps)),
        grid=(2 * sub,),
        in_specs=half + half + [one, one, square, square] + [double] * len(sofar) + [pl.BlockSpec(memory_space=pl.ANY)] * len(deps),
        out_specs=[row] + half + [row, double],
        out_shape=[
            jax.ShapeDtypeStruct((count, width), BF16),
            jax.ShapeDtypeStruct((shard, width), BF16),
            jax.ShapeDtypeStruct((shard, width), BF16),
            jax.ShapeDtypeStruct((count, width), BF16),
            jax.ShapeDtypeStruct((width, 2 * hid), BF16 if sofar else F32),
        ],
        scratch_shapes=[pltpu.VMEM((width, 2 * hid), F32)] * len(sofar),
        compiler_params=params(),
        cost_estimate=cost(8),
        name="feed_forward",
    )(*toks, *grads, gain, bias, w_up, w_down_t, *sofar, *deps)


def assemble_kernel(me, part_a, part_b, part_c, part_d, out, last, whole):
    rows = part_a.shape[0]
    for k, part in enumerate((part_a, part_b, part_c, part_d)):
        whole[pl.ds(pl.multiple_of(jnp.bitwise_xor(me[0], k) * rows, rows), rows)] = part[...]
    turned = whole[...].T
    out[...] = turned
    last[...] = turned[3 * last.shape[0] :]


def assemble(me, parts):
    rows, width = parts[0].shape
    return pl.pallas_call(
        assemble_kernel,
        grid_spec=pltpu.PrefetchScalarGridSpec(
            num_scalar_prefetch=1,
            grid=(1,),
            in_specs=[pl.BlockSpec((rows, width), lambda b, m: (0, 0))] * 4,
            out_specs=[
                pl.BlockSpec((width, 4 * rows), lambda b, m: (0, 0)),
                pl.BlockSpec((width // 4, 4 * rows), lambda b, m: (0, 0)),
            ],
            scratch_shapes=[pltpu.VMEM((4 * rows, width), BF16)],
        ),
        out_shape=[
            jax.ShapeDtypeStruct((width, 4 * rows), BF16),
            jax.ShapeDtypeStruct((width // 4, 4 * rows), BF16),
        ],
        compiler_params=params(),
        cost_estimate=cost(3),
        name="assemble",
    )(me, *parts)


def project_kernel(me, n_a, n_b, g_a, g_b, g_c, g_d, wat, cosine, sine, qkv, d_ctx):
    low = of_list([n_a, n_b])
    width = d_ctx.shape[0]
    out = dot_nt(wat[: 3 * width], low)
    d_ctx[...] = dot_nt(wat[3 * width :], of_list([g_a, g_b, g_c, g_d])).astype(BF16)
    cos_b, sin_b = cosine[...], sine[...]
    scale = HEAD_DIM ** (-0.5)
    qkv[:width] = (rope_t(out[:width], cos_b, sin_b) * scale).astype(BF16)
    qkv[width : 2 * width] = rope_t(out[width : 2 * width], cos_b, sin_b).astype(BF16)
    qkv[2 * width :] = out[2 * width :].astype(BF16)


def project(me, normeds, grads, wat, cosine, sine, deps=(), block=384):
    shard, width = grads[0].shape
    total = cosine.shape[1]
    sub = shard // block
    own = width // 4
    place = placing(0, sub)
    table = pl.BlockSpec((HALF_ROT, block), lambda b, m: (0, place(b, m)))
    return pl.pallas_call(
        waiting(project_kernel, 1, 9, len(deps)),
        grid_spec=pltpu.PrefetchScalarGridSpec(
            num_scalar_prefetch=1,
            grid=(4 * sub,),
            in_specs=list_specs(block, width, 2 * sub, 2)
            + list_specs(block, width, sub, 4)
            + [pl.BlockSpec((4 * own, width), lambda b, m: (0, 0)), table, table]
            + [pl.BlockSpec(memory_space=pl.ANY)] * len(deps),
            out_specs=[
                pl.BlockSpec((3 * own, block), lambda b, m: (0, place(b, m))),
                pl.BlockSpec((own, block), lambda b, m: (0, place(b, m))),
            ],
        ),
        out_shape=[
            jax.ShapeDtypeStruct((3 * own, total), BF16),
            jax.ShapeDtypeStruct((own, total), BF16),
        ],
        compiler_params=params(),
        cost_estimate=cost(11),
        name="project",
    )(me, *normeds, *grads, wat, cosine, sine, *deps)


def attention_kernel(low_block, me, qkv, d_ctx, begin, cosine, sine, ctx_a, ctx_b, ctx_c, ctx_d, dq, kv, k_rows, v_rows, k_t, v_t, dk_t, dv_t):
    i = pl.program_id(0)
    width = d_ctx.shape[0]
    heads = width // HEAD_DIM
    here = pl.multiple_of(i * QB, QB)
    q_t = qkv[:width]
    k_here = qkv[width : 2 * width]
    v_here = qkv[2 * width :]
    k_t[:, pl.ds(here, QB)] = k_here
    v_t[:, pl.ds(here, QB)] = v_here
    k_nat = k_here.T
    v_nat = v_here.T
    for h in range(heads):
        cols = slice(h * HEAD_DIM, (h + 1) * HEAD_DIM)
        k_rows[h, pl.ds(here, QB), :] = k_nat[:, cols]
        v_rows[h, pl.ds(here, QB), :] = v_nat[:, cols]
    dk_t[:, pl.ds(here, QB)] = jnp.zeros((width, QB), F32)
    dv_t[:, pl.ds(here, QB)] = jnp.zeros((width, QB), F32)
    base = low_block[i]
    start = pl.multiple_of(base * QB, QB)
    reach = i - base
    first_key = begin[...] - start
    last_key = lax.broadcasted_iota(jnp.int32, (1, QB), 1) + (here - start)
    do_t = d_ctx[...]
    cos_here = cosine[:, pl.ds(here, QB)]
    sin_here = sine[:, pl.ds(here, QB)]
    scale = HEAD_DIM ** (-0.5)

    def run(blocks):
        span = blocks * QB
        key = lax.broadcasted_iota(jnp.int32, (span, QB), 0)
        allowed = (key >= first_key) & (key <= last_key)
        window = pl.ds(start, span)
        contexts = []
        for h in range(heads):
            rows = slice(h * HEAD_DIM, (h + 1) * HEAD_DIM)
            scores = dot_nn(k_rows[h, window, :], q_t[rows])
            scores = jnp.where(allowed, scores, MASKED)
            highest = jnp.max(scores, axis=0, keepdims=True)
            expo = jnp.exp(scores - highest)
            prob = expo * (1.0 / jnp.sum(expo, axis=0, keepdims=True))
            prob_low = prob.astype(BF16)
            context = dot_nn(v_t[rows, window], prob_low)
            d_prob = dot_nn(v_rows[h, window, :], do_t[rows])
            delta = jnp.sum(do_t[rows].astype(F32) * context, axis=0, keepdims=True)
            d_scores = (prob * (d_prob - delta)).astype(BF16)
            dq_h = dot_nn(k_t[rows, window], d_scores) * scale
            dq[rows] = rope_t(dq_h, cos_here, -sin_here).astype(BF16)
            contexts.append(context.astype(BF16))
            dk_t[rows, window] += dot_nt(q_t[rows], d_scores)
            dv_t[rows, window] += dot_nt(do_t[rows], prob_low)
        for j, ctx in enumerate((ctx_a, ctx_b, ctx_c, ctx_d)):

            @pl.when(i // (pl.num_programs(0) // 4) == jnp.bitwise_xor(me[0], j))
            def _():
                ctx[...] = jnp.concatenate(contexts, axis=0)

    for far in range(SEQ_MAX // QB + 1):
        pl.when(reach == far)(partial(run, far + 1))

    @pl.when(i == pl.num_programs(0) - 1)
    def _():
        kv[:width] = rope_t(dk_t[...], cosine[...], -sine[...]).astype(BF16)
        kv[width:] = dv_t[...].astype(BF16)


def attention(low_block, me, qkv, d_ctx, begin, cosine, sine, deps=()):
    width, total = d_ctx.shape
    heads = width // HEAD_DIM

    part = total // QB // 4

    def column(rows):
        return pl.BlockSpec((rows, QB), lambda i, m, r: (0, i))

    def whole(rows):
        return pl.BlockSpec((rows, total), lambda i, m, r: (0, 0))

    shards = [
        pl.BlockSpec(
            (width, QB),
            lambda i, m, r, j=j: (0, jnp.clip(i - jnp.bitwise_xor(r[0], j) * part, 0, part - 1)),
        )
        for j in range(4)
    ]

    return pl.pallas_call(
        waiting(attention_kernel, 2, 5, len(deps)),
        grid_spec=pltpu.PrefetchScalarGridSpec(
            num_scalar_prefetch=2,
            grid=(total // QB,),
            in_specs=[
                column(3 * width),
                column(width),
                column(1),
                whole(HALF_ROT),
                whole(HALF_ROT),
            ]
            + [pl.BlockSpec(memory_space=pl.ANY)] * len(deps),
            out_specs=shards + [column(width), whole(2 * width)],
            scratch_shapes=[
                pltpu.VMEM((heads, total, HEAD_DIM), BF16),
                pltpu.VMEM((heads, total, HEAD_DIM), BF16),
                pltpu.VMEM((width, total), BF16),
                pltpu.VMEM((width, total), BF16),
                pltpu.VMEM((width, total), F32),
                pltpu.VMEM((width, total), F32),
            ],
        ),
        out_shape=[jax.ShapeDtypeStruct((width, total // 4), BF16)] * 4
        + [
            jax.ShapeDtypeStruct((width, total), BF16),
            jax.ShapeDtypeStruct((2 * width, total), BF16),
        ],
        compiler_params=params(),
        cost_estimate=cost(46),
        name="attention",
    )(low_block, me, qkv, d_ctx, begin, cosine, sine, *deps)


def finish_kernel(last, me, *refs):
    ctx_a, ctx_b, dq, kv, tok_a, tok_b, g_a, g_b, normed, d_mlp, wat = refs[:11]
    if last:
        sums_in, total_in, dn_a, dn_b, sums, weight_g, total_g = refs[11:]
    else:
        dn_a, dn_b, sums, total_g = refs[11:]

    @pl.when(pl.program_id(0) == 0)
    def _():
        sums[...] = sums_in[...] if last else jnp.zeros_like(sums)
        total_g[...] = total_in[...] if last else jnp.zeros_like(total_g)

    own = dq.shape[0]
    n = normed[...]
    total = dot_nn(dq[...].T, wat[:own]) + dot_nn(kv[...].T, wat[own : 3 * own])
    total_g[:own] += dot_nn(dq[...], n)
    total_g[own : 3 * own] += dot_nn(kv[...], n)
    total_g[3 * own :] += dot_nn(of_list([ctx_a, ctx_b]), of_list([g_a, g_b]))
    total = total + d_mlp[...].astype(F32)
    unit, _ = unit_of(of_list([tok_a, tok_b]))
    sums[0:1] += jnp.sum(total * unit, axis=0, keepdims=True)
    sums[1:2] += jnp.sum(total, axis=0, keepdims=True)
    put_list([dn_a, dn_b], total.astype(BF16))
    if last:

        @pl.when(pl.program_id(0) == pl.num_programs(0) - 1)
        def _():
            weight_g[...] = total_g[...].T


def finish(me, ctxs, dq, kv, toks, grads, normed, d_mlp, wat, first, sofar=(), deps=(), block=384):
    shard, width = toks[0].shape
    sub = shard // block
    place = placing(first, sub)
    last = len(sofar) > 0

    def column(rows):
        return pl.BlockSpec((rows, block), lambda b, m: (0, place(b, m)))

    context = [
        pl.BlockSpec((width // 4, block), lambda b, m, k=k: (0, jnp.clip(b - k * sub, 0, sub - 1)))
        for k in range(2)
    ]
    two = list_specs(block, width, sub, 2)
    row = pl.BlockSpec((block, width), lambda b, m: (b, 0))
    square = pl.BlockSpec((width, width), lambda b, m: (0, 0))
    sums = pl.BlockSpec((8, width), lambda b, m: (0, 0))
    return pl.pallas_call(
        waiting(partial(finish_kernel, last), 1, 11 + len(sofar), len(deps)),
        grid_spec=pltpu.PrefetchScalarGridSpec(
            num_scalar_prefetch=1,
            grid=(2 * sub,),
            in_specs=context
            + [column(width // 4), column(width // 2)]
            + two
            + two
            + [row, row, square]
            + ([sums, square] if last else [])
            + [pl.BlockSpec(memory_space=pl.ANY)] * len(deps),
            out_specs=two + [sums, square],
            scratch_shapes=[pltpu.VMEM((width, width), F32)] if last else [],
        ),
        out_shape=[jax.ShapeDtypeStruct((shard, width), BF16)] * 2
        + [jax.ShapeDtypeStruct((8, width), F32), jax.ShapeDtypeStruct((width, width), F32)],
        compiler_params=params(),
        cost_estimate=cost(10),
        name="finish",
    )(me, *ctxs, dq, kv, *toks, *grads, normed, d_mlp, wat, *sofar, *deps)


def input_gradient_kernel(tok, cotangent, dn_a, dn_b, dn_c, gain, out):
    share = dn_a[...].astype(F32) + dn_b[...].astype(F32) + dn_c[...].astype(F32)
    unit, inv_std = unit_of(tok[...])
    unit_grad = share * gain[...]
    plain_mean = jnp.mean(unit_grad, axis=1, keepdims=True)
    cross_mean = jnp.mean(unit_grad * unit, axis=1, keepdims=True)
    out[...] = (
        cotangent[...].astype(F32) + inv_std * (unit_grad - plain_mean - unit * cross_mean)
    ).astype(BF16)


def input_gradient(tok, cotangent, dns, gain, deps=(), block=256):
    shard, width = tok.shape
    row = pl.BlockSpec((block, width), lambda b: (b, 0))
    return pl.pallas_call(
        waiting(input_gradient_kernel, 0, 6, len(deps)),
        grid=(shard // block,),
        in_specs=[row] * 5
        + [pl.BlockSpec((1, width), lambda b: (0, 0))]
        + [pl.BlockSpec(memory_space=pl.ANY)] * len(deps),
        out_specs=row,
        out_shape=jax.ShapeDtypeStruct((shard, width), BF16),
        compiler_params=params(),
        cost_estimate=cost(5),
        name="input_gradient",
    )(tok, cotangent, *dns, gain, *deps)


def mix_kernel(tok, mlp_a, mlp_b, mlp_c, *rest):
    ctxs, weights, mixed = rest[:4], rest[4:8], rest[8]
    total = tok[...].astype(F32) + mlp_a[...].astype(F32)
    total = total + (mlp_b[...].astype(F32) + mlp_c[...].astype(F32))
    for ctx, weight in zip(ctxs, weights):
        total = total + dot_nn(ctx[...].T, weight[...])
    mixed[...] = total.astype(BF16)


def mix(tok, mlps, ctxs, weights, deps=(), block=384):
    shard, width = tok.shape
    own = width // 4
    row = pl.BlockSpec((block, width), lambda b: (b, 0))
    return pl.pallas_call(
        waiting(mix_kernel, 0, 12, len(deps)),
        grid=(shard // block,),
        in_specs=[row] * 4
        + [pl.BlockSpec((own, block), lambda b: (0, b))] * 4
        + [pl.BlockSpec((own, width), lambda b: (0, 0))] * 4
        + [pl.BlockSpec(memory_space=pl.ANY)] * len(deps),
        out_specs=row,
        out_shape=jax.ShapeDtypeStruct((shard, width), BF16),
        compiler_params=params(),
        cost_estimate=cost(5),
        name="mix",
    )(tok, *mlps, *ctxs, *weights, *deps)


def together(*values, deps=()):
    def nothing(*refs):
        pass

    anywhere = pl.BlockSpec(memory_space=pl.ANY)
    return pl.pallas_call(
        nothing,
        in_specs=[anywhere] * (len(values) + len(deps)),
        out_specs=[anywhere] * len(values),
        out_shape=[jax.ShapeDtypeStruct(value.shape, value.dtype) for value in values],
        input_output_aliases={k: k for k in range(len(values))},
        cost_estimate=cost(1),
        name="together",
    )(*values, *deps)


def after(value, *deps):
    return together(value, deps=deps)[0]


def swap(value, axis, size, bit):
    return lax.ppermute(value, axis, [(i, i ^ bit) for i in range(size)])


def bits_of(size):
    out, bit = [], 1
    while bit < size:
        out.insert(0, bit)
        bit *= 2
    return out


class Gather:
    def __init__(self, shard, size, me):
        self.held, self.done, self.size, self.me = shard, [], size, me

    def send(self, bit):
        self.bit = bit
        self.theirs = swap(self.held, "dp", self.size, bit)

    def whole(self):
        return self.held.reshape(-1, self.held.shape[-1])


def merge_kernel(second, *refs):
    count = len(refs) // 3
    for k in range(count):
        held, theirs, out = refs[2 * k], refs[2 * k + 1], refs[2 * count + k]
        for high in range(held.shape[0]):
            out[high, second[k]] = held[high]
            out[high, 1 - second[k]] = theirs[high]


def merge(gathers, deps=()):
    second, parts, shapes = [], [], []
    for gather in gathers:
        second.append(((gather.me & gather.bit) != 0).astype(jnp.int32))
        high = 2 ** sum(1 for other in gather.done if other > gather.bit)
        gather.done.append(gather.bit)
        width = gather.held.shape[-1]
        one = (high, gather.held.size // (high * width), width)
        parts += [gather.held.reshape(one), gather.theirs.reshape(one)]
        shapes.append(jax.ShapeDtypeStruct((one[0], 2, *one[1:]), gather.held.dtype))

    def whole(shape):
        return pl.BlockSpec(shape, lambda b, m: (0,) * len(shape))

    outs = pl.pallas_call(
        waiting(merge_kernel, 1, len(parts), len(deps)),
        grid_spec=pltpu.PrefetchScalarGridSpec(
            num_scalar_prefetch=1,
            grid=(1,),
            in_specs=[whole(part.shape) for part in parts]
            + [pl.BlockSpec(memory_space=pl.ANY)] * len(deps),
            out_specs=[whole(shape.shape) for shape in shapes],
        ),
        out_shape=shapes,
        compiler_params=params(),
        cost_estimate=cost(2),
        name="merge",
    )(jnp.stack(second), *parts, *deps)
    for gather, out in zip(gathers, outs):
        gather.held = out


class Scatter:
    def __init__(self, whole, size, me):
        rows, width = whole.shape
        self.left, self.size, self.me = bits_of(size), size, me
        self.held = whole.reshape((2,) * len(self.left) + (rows // size, width))

    def send(self, bit, deps=()):
        axis = self.left.index(bit)
        self.left.remove(bit)
        mine = ((self.me & bit) != 0).astype(jnp.int32)
        self.keep = lax.dynamic_index_in_dim(self.held, mine, axis, keepdims=False)
        away = lax.dynamic_index_in_dim(self.held, 1 - mine, axis, keepdims=False)
        self.away = away.astype(BF16)
        if deps:
            self.away = after(self.away, *deps)
        self.theirs = swap(self.away, "dp", self.size, bit)

    def take(self):
        self.held = self.keep.astype(F32) + self.theirs.astype(F32)

    def send_last(self):
        high, low = self.left
        quarters = self.held.reshape(4, *self.held.shape[2:])
        place = (self.me // low) % 4
        self.keep = lax.dynamic_index_in_dim(quarters, place, 0, keepdims=False).astype(F32)
        self.aways = [
            lax.dynamic_index_in_dim(quarters, place ^ k, 0, keepdims=False).astype(BF16)
            for k in range(1, 4)
        ]
        self.parts = [swap(self.aways[k - 1], "dp", self.size, k * low) for k in range(1, 4)]

    def take_last(self):
        one, two, three = [part.astype(F32) for part in self.parts]
        self.held = (self.keep + one) + (two + three)


def sum_over(value, axis, size, bits):
    if len(bits) == 1:
        return value + swap(value, axis, size, bits[0])
    far, near = bits
    parts = together(*[swap(value, axis, size, bit) for bit in (near, far, far + near)])
    return (value + parts[0]) + (parts[1] + parts[2])


def tables(lengths, count):
    doc_ends = jnp.cumsum(lengths)
    places = jnp.arange(count, dtype=jnp.int32)
    after_end = places[:, None] >= doc_ends[None, :]
    begins = jnp.max(jnp.where(after_end, doc_ends[None, :], 0), axis=1)
    offset_f = (places - begins).astype(F32)
    frequency = jnp.exp(
        -(2.0 * jnp.arange(HALF_ROT, dtype=F32) / ROT_DIM) * math.log(10000.0)
    )
    angle = frequency[:, None] * offset_f[None, :]
    low_block = begins.reshape(count // QB, QB)[:, 0] // QB
    return begins[None, :], low_block, jnp.cos(angle), jnp.sin(angle)


def body(
    n_dp, n_row, tokens, ln_gain, ln_bias, w_query, w_key, w_value, w_out, w_up, w_down, doc_lengths, cotangent
):
    shard, width = tokens.shape
    total = shard * n_row
    own = width // n_row
    hid = w_up.shape[1]
    dp_me = lax.axis_index("dp")
    row_me = lax.axis_index("row").astype(jnp.int32)
    me = row_me.reshape(1)
    bits = bits_of(n_dp)
    to_core = partial(swap, axis="row", size=n_row, bit=1)
    to_chip = partial(swap, axis="row", size=n_row, bit=2)
    to_both = partial(swap, axis="row", size=n_row, bit=3)

    tok = [tokens, to_core(tokens), to_chip(tokens)]
    grad = [cotangent, to_core(cotangent)]
    up = Gather(w_up, n_dp, dp_me)
    down = Gather(w_down.T, n_dp, dp_me)
    orders = list(zip(bits, bits[-1:] + bits[:-1]))
    attn_shard = jnp.concatenate([w_query, w_key, w_value, w_out.T], axis=1)
    attn = Gather(attn_shard, n_dp, dp_me)
    for k, (first, second) in enumerate(orders):
        up.send(first)
        down.send(second)
        if k == 0:
            for bit in bits[:1:-1]:
                attn.send(bit)
                attn_ready = attn.theirs
                merge([attn])
        merge([up, down], (attn_ready, tok[2]) if k + 2 == len(orders) else ())
    grad.append(to_chip(cotangent))
    begin, low_block, cosine, sine = tables(doc_lengths[0], total)
    gain, bias = ln_gain[None, :], ln_bias[None, :]

    up_w, down_w = up.whole(), down.whole()
    quarter = attn.whole()
    quarters = [swap(quarter, "dp", n_dp, bit) for bit in (bits[1], bits[0], bits[0] + bits[1])]
    near_n, *near_mlp, near_dm, ffn_g = feed_forward(
        tok[:2], grad[:2], gain, bias, up_w, down_w, (), (quarter, cosine, sine, begin)
    )
    tok.append(to_core(after(tok[2], near_dm, *quarters)))
    grad[2] = after(grad[2], near_dm, *quarters)
    grad.append(to_core(grad[2]))
    wat, own_out = assemble((dp_me // bits[1]).astype(jnp.int32).reshape(1), [quarter, *quarters])
    far_n, *far_mlp, far_dm, ffn_g = feed_forward(
        tok[2:], grad[2:], gain, bias, up_w, down_w, (ffn_g,), (wat,)
    )
    ffn_wg = lax.psum_scatter(ffn_g, "dp", scatter_dimension=0, tiled=True)
    far_mlp_core = to_core(far_mlp[1])
    near_mlp_core = to_core(near_mlp[1])

    qkv, d_ctx = project(me, [near_n, far_n], grad, wat, cosine, sine)
    mlp_both = (far_mlp[0].astype(F32) + far_mlp_core.astype(F32)).astype(BF16)
    mlp_chip = to_chip(mlp_both)
    out_w = [own_out]
    out_w += [to_core(out_w[0]), to_chip(out_w[0]), to_both(out_w[0])]

    *ctx, dq, kv = attention(
        low_block, me, qkv, d_ctx, begin, cosine, sine, (mlp_both,)
    )

    ctxs = [ctx[0], to_core(ctx[1]), to_chip(ctx[2]), to_both(ctx[3])]
    far_dn, far_dn_b, *sofar = finish(
        me, ctx[2:], dq, kv, tok[2:], grad[2:], far_n, far_dm, wat, 2, (), (mlp_chip, *out_w[1:])
    )
    theirs = to_core(far_dn_b)
    both = (far_dn.astype(F32) + theirs.astype(F32)).astype(BF16)
    dn_chip = to_chip(both)
    near_dn, near_dn_b, sums, attn_g = finish(
        me, ctx[:2], dq, kv, tok[:2], grad[:2], near_n, near_dm, wat, 0, sofar,
        (both, ctxs[2], ctxs[3], ffn_wg),
    )
    dn_core = to_core(near_dn_b)
    attn_sum = Scatter(attn_g, n_dp, dp_me)
    for bit in bits[:2:-1]:
        attn_sum.send(bit)
        attn_sum.take()
        sums = sum_over(sums, "dp", n_dp, [bit])
    first = swap(sums, "dp", n_dp, bits[2])
    attn_sum.send(bits[2], (first,))
    sums = sum_over(sums + first, "dp", n_dp, bits[:2])
    sums = sum_over(sums, "row", n_row, [2, 1])
    mixed = mix(tokens, [near_mlp[0], near_mlp_core, mlp_chip], ctxs, out_w)
    attn_sum.theirs = after(attn_sum.theirs, sums, dn_chip, mixed)
    attn_sum.take()
    attn_sum.send_last()
    input_grad = input_gradient(
        tokens, cotangent, [near_dn, dn_core, dn_chip], gain, attn_sum.aways
    )
    attn_sum.parts[0] = after(attn_sum.parts[0], input_grad)
    attn_sum.take_last()

    attn_wg, ffn_wg = attn_sum.held, ffn_wg.astype(F32)
    return (
        mixed,
        input_grad,
        sums[0],
        sums[1],
        attn_wg[:, :own],
        attn_wg[:, own : 2 * own],
        attn_wg[:, 2 * own : 3 * own],
        attn_wg[:, 3 * own :].T,
        ffn_wg[:, :hid],
        ffn_wg[:, hid:].T,
    )


def solution(mesh):
    in_specs = (
        P(("dp", "row"), None),
        P(),
        P(),
        P("dp", "row"),
        P("dp", "row"),
        P("dp", "row"),
        P("row", "dp"),
        P("dp", "row"),
        P("row", "dp"),
        P("dp", None),
        P(("dp", "row"), None),
    )
    out_specs = (
        P(("dp", "row"), None),
        P(("dp", "row"), None),
        P(),
        P(),
        P("dp", "row"),
        P("dp", "row"),
        P("dp", "row"),
        P("row", "dp"),
        P("dp", "row"),
        P("row", "dp"),
    )
    sizes = (mesh.shape["dp"], mesh.shape["row"])
    return jax.shard_map(
        partial(body, *sizes), mesh=mesh, in_specs=in_specs, out_specs=out_specs, check_vma=False
    )
```

```python
from functools import partial
import math

import jax
import jax.numpy as jnp
from jax import lax
from jax.experimental import pallas as pl
from jax.experimental.pallas import tpu as pltpu
from jax.sharding import PartitionSpec as P

HEAD_DIM = 64
ROT_DIM = 16
HALF_ROT = ROT_DIM // 2
SEQ_MAX = 1024
QB = 256
EPS = 1e-05
MASKED = -1000000000.0
MIB = 1024 * 1024
F32 = jnp.float32
BF16 = jnp.bfloat16


def dot_nn(a, b):
    return lax.dot_general(a, b, (((1,), (0,)), ((), ())), preferred_element_type=F32)


def dot_nt(a, b):
    return lax.dot_general(a, b, (((1,), (1,)), ((), ())), preferred_element_type=F32)


def dot_tn(a, b):
    return lax.dot_general(a, b, (((0,), (0,)), ((), ())), preferred_element_type=F32)


def unit_of(rows):
    inputs = rows.astype(F32)
    average = jnp.mean(inputs, axis=1, keepdims=True)
    centered = inputs - average
    spread_sq = jnp.mean(centered * centered, axis=1, keepdims=True)
    inv_std = lax.rsqrt(spread_sq + EPS)
    return centered * inv_std, inv_std


def rope_t(field, cosine, sine):
    heads = field.shape[0] // HEAD_DIM
    pieces = []
    for h in range(heads):
        one = field[h * HEAD_DIM : (h + 1) * HEAD_DIM]
        first, second = one[:HALF_ROT], one[HALF_ROT:ROT_DIM]
        pieces += [
            first * cosine - second * sine,
            second * cosine + first * sine,
            one[ROT_DIM:],
        ]
    return jnp.concatenate(pieces, axis=0)


def params(limit=56):
    return pltpu.CompilerParams(vmem_limit_bytes=limit * MIB)


def placing(first, sub):
    def place(b, me_ref):
        return jnp.bitwise_xor(me_ref[0], first + b // sub) * sub + b % sub

    return place


def list_specs(block, width, sub, count):
    return [
        pl.BlockSpec((block, width), lambda b, m, k=k: (jnp.clip(b - k * sub, 0, sub - 1), 0))
        for k in range(count)
    ]


def waiting(kernel, scalars, operands, deps):
    ahead = scalars + operands

    def run(*refs):
        kernel(*refs[:ahead], *refs[ahead + deps :])

    return run


def of_list(refs):
    part = pl.num_programs(0) // len(refs)
    out = refs[0][...]
    for k in range(1, len(refs)):
        out = jnp.where(pl.program_id(0) >= k * part, refs[k][...], out)
    return out


def put_list(refs, value):
    part = pl.num_programs(0) // len(refs)
    for k, ref in enumerate(refs):

        @pl.when(pl.program_id(0) // part == k)
        def _():
            ref[...] = value


def cost(micros):
    return pl.CostEstimate(flops=int(micros * 9.612e+07), bytes_accessed=1, transcendentals=0)


def ffn_kernel(tok_a, tok_b, g_a, g_b, gain, bias, w_up, w_down_t, *rest):
    hid = w_up.shape[1]
    last = len(rest) > 5
    if last:
        sofar, normed, mlp_a, mlp_b, d_normed, weight_out, weight_g = rest
    else:
        normed, mlp_a, mlp_b, d_normed, weight_g = rest

    @pl.when(pl.program_id(0) == 0)
    def _():
        weight_g[...] = sofar[...] if last else jnp.zeros_like(weight_g)

    unit, _ = unit_of(of_list([tok_a, tok_b]))
    n, g = (unit * gain[...] + bias[...]).astype(BF16), of_list([g_a, g_b])
    normed[...] = n
    up_pre = dot_nn(n, w_up[...])
    d_hidden = dot_nn(g, w_down_t[...])
    cdf = 0.5 * (1.0 + lax.erf(up_pre * (2.0**-0.5)))
    pdf = jnp.exp(-0.5 * up_pre * up_pre) * ((2.0 * math.pi) ** -0.5)
    hidden = (up_pre * cdf).astype(BF16)
    d_up = (d_hidden * (cdf + up_pre * pdf)).astype(BF16)
    branch = dot_nt(hidden, w_down_t[...]).astype(BF16)
    d_normed[...] = dot_nt(d_up, w_up[...]).astype(BF16)
    weight_g[:, :hid] += dot_tn(n, d_up)
    weight_g[:, hid:] += dot_tn(g, hidden)
    put_list([mlp_a, mlp_b], branch)
    if last:

        @pl.when(pl.program_id(0) == pl.num_programs(0) - 1)
        def _():
            weight_out[...] = weight_g[...].astype(BF16)


def feed_forward(toks, grads, gain, bias, w_up, w_down_t, sofar, deps=(), block=384):
    shard, width = grads[0].shape
    count = 2 * shard
    hid = w_up.shape[1]
    sub = shard // block
    row = pl.BlockSpec((block, width), lambda b: (b, 0))
    half = [
        pl.BlockSpec((block, width), lambda b, k=k: (jnp.clip(b - k * sub, 0, sub - 1), 0))
        for k in range(2)
    ]
    one = pl.BlockSpec((1, width), lambda b: (0, 0))
    square = pl.BlockSpec((width, hid), lambda b: (0, 0))
    double = pl.BlockSpec((width, 2 * hid), lambda b: (0, 0))
    return pl.pallas_call(
        waiting(ffn_kernel, 0, 8 + len(sofar), len(deps)),
        grid=(2 * sub,),
        in_specs=half + half + [one, one, square, square] + [double] * len(sofar) + [pl.BlockSpec(memory_space=pl.ANY)] * len(deps),
        out_specs=[row] + half + [row, double],
        out_shape=[
            jax.ShapeDtypeStruct((count, width), BF16),
            jax.ShapeDtypeStruct((shard, width), BF16),
            jax.ShapeDtypeStruct((shard, width), BF16),
            jax.ShapeDtypeStruct((count, width), BF16),
            jax.ShapeDtypeStruct((width, 2 * hid), BF16 if sofar else F32),
        ],
        scratch_shapes=[pltpu.VMEM((width, 2 * hid), F32)] * len(sofar),
        compiler_params=params(),
        cost_estimate=cost(8),
        name="feed_forward",
    )(*toks, *grads, gain, bias, w_up, w_down_t, *sofar, *deps)


def assemble_kernel(me, part_a, part_b, part_c, part_d, out, last, whole):
    rows = part_a.shape[0]
    for k, part in enumerate((part_a, part_b, part_c, part_d)):
        whole[pl.ds(pl.multiple_of(jnp.bitwise_xor(me[0], k) * rows, rows), rows)] = part[...]
    turned = whole[...].T
    out[...] = turned
    last[...] = turned[3 * last.shape[0] :]


def assemble(me, parts):
    rows, width = parts[0].shape
    return pl.pallas_call(
        assemble_kernel,
        grid_spec=pltpu.PrefetchScalarGridSpec(
            num_scalar_prefetch=1,
            grid=(1,),
            in_specs=[pl.BlockSpec((rows, width), lambda b, m: (0, 0))] * 4,
            out_specs=[
                pl.BlockSpec((width, 4 * rows), lambda b, m: (0, 0)),
                pl.BlockSpec((width // 4, 4 * rows), lambda b, m: (0, 0)),
            ],
            scratch_shapes=[pltpu.VMEM((4 * rows, width), BF16)],
        ),
        out_shape=[
            jax.ShapeDtypeStruct((width, 4 * rows), BF16),
            jax.ShapeDtypeStruct((width // 4, 4 * rows), BF16),
        ],
        compiler_params=params(),
        cost_estimate=cost(3),
        name="assemble",
    )(me, *parts)


def project_kernel(me, n_a, n_b, g_a, g_b, g_c, g_d, wat, cosine, sine, qkv, d_ctx):
    low = of_list([n_a, n_b])
    width = d_ctx.shape[0]
    out = dot_nt(wat[: 3 * width], low)
    d_ctx[...] = dot_nt(wat[3 * width :], of_list([g_a, g_b, g_c, g_d])).astype(BF16)
    cos_b, sin_b = cosine[...], sine[...]
    scale = HEAD_DIM ** (-0.5)
    qkv[:width] = (rope_t(out[:width], cos_b, sin_b) * scale).astype(BF16)
    qkv[width : 2 * width] = rope_t(out[width : 2 * width], cos_b, sin_b).astype(BF16)
    qkv[2 * width :] = out[2 * width :].astype(BF16)


def project(me, normeds, grads, wat, cosine, sine, deps=(), block=384):
    shard, width = grads[0].shape
    total = cosine.shape[1]
    sub = shard // block
    own = width // 4
    place = placing(0, sub)
    table = pl.BlockSpec((HALF_ROT, block), lambda b, m: (0, place(b, m)))
    return pl.pallas_call(
        waiting(project_kernel, 1, 9, len(deps)),
        grid_spec=pltpu.PrefetchScalarGridSpec(
            num_scalar_prefetch=1,
            grid=(4 * sub,),
            in_specs=list_specs(block, width, 2 * sub, 2)
            + list_specs(block, width, sub, 4)
            + [pl.BlockSpec((4 * own, width), lambda b, m: (0, 0)), table, table]
            + [pl.BlockSpec(memory_space=pl.ANY)] * len(deps),
            out_specs=[
                pl.BlockSpec((3 * own, block), lambda b, m: (0, place(b, m))),
                pl.BlockSpec((own, block), lambda b, m: (0, place(b, m))),
            ],
        ),
        out_shape=[
            jax.ShapeDtypeStruct((3 * own, total), BF16),
            jax.ShapeDtypeStruct((own, total), BF16),
        ],
        compiler_params=params(),
        cost_estimate=cost(11),
        name="project",
    )(me, *normeds, *grads, wat, cosine, sine, *deps)


def attention_kernel(low_block, me, qkv, d_ctx, begin, cosine, sine, ctx_a, ctx_b, ctx_c, ctx_d, dq, kv, k_rows, v_rows, k_t, v_t, dk_t, dv_t):
    i = pl.program_id(0)
    width = d_ctx.shape[0]
    heads = width // HEAD_DIM
    here = pl.multiple_of(i * QB, QB)
    q_t = qkv[:width]
    k_here = qkv[width : 2 * width]
    v_here = qkv[2 * width :]
    k_t[:, pl.ds(here, QB)] = k_here
    v_t[:, pl.ds(here, QB)] = v_here
    k_nat = k_here.T
    v_nat = v_here.T
    for h in range(heads):
        cols = slice(h * HEAD_DIM, (h + 1) * HEAD_DIM)
        k_rows[h, pl.ds(here, QB), :] = k_nat[:, cols]
        v_rows[h, pl.ds(here, QB), :] = v_nat[:, cols]
    dk_t[:, pl.ds(here, QB)] = jnp.zeros((width, QB), F32)
    dv_t[:, pl.ds(here, QB)] = jnp.zeros((width, QB), F32)
    base = low_block[i]
    start = pl.multiple_of(base * QB, QB)
    reach = i - base
    first_key = begin[...] - start
    last_key = lax.broadcasted_iota(jnp.int32, (1, QB), 1) + (here - start)
    do_t = d_ctx[...]
    cos_here = cosine[:, pl.ds(here, QB)]
    sin_here = sine[:, pl.ds(here, QB)]
    scale = HEAD_DIM ** (-0.5)

    def run(blocks):
        span = blocks * QB
        key = lax.broadcasted_iota(jnp.int32, (span, QB), 0)
        allowed = (key >= first_key) & (key <= last_key)
        window = pl.ds(start, span)
        contexts = []
        head_rows = [slice(h * HEAD_DIM, (h + 1) * HEAD_DIM) for h in range(heads)]
        all_scores = [dot_nn(k_rows[h, window, :], q_t[rows]) for h, rows in enumerate(head_rows)]
        all_d_prob = [dot_nn(v_rows[h, window, :], do_t[rows]) for h, rows in enumerate(head_rows)]
        for h, rows in enumerate(head_rows):
            scores = jnp.where(allowed, all_scores[h], MASKED)
            highest = jnp.max(scores, axis=0, keepdims=True)
            expo = jnp.exp(scores - highest)
            prob = expo * (1.0 / jnp.sum(expo, axis=0, keepdims=True))
            prob_low = prob.astype(BF16)
            context = dot_nn(v_t[rows, window], prob_low)
            delta = jnp.sum(do_t[rows].astype(F32) * context, axis=0, keepdims=True)
            d_scores = (prob * (all_d_prob[h] - delta)).astype(BF16)
            dq_h = dot_nn(k_t[rows, window], d_scores) * scale
            dq[rows] = rope_t(dq_h, cos_here, -sin_here).astype(BF16)
            contexts.append(context.astype(BF16))
            dk_t[rows, window] += dot_nt(q_t[rows], d_scores)
            dv_t[rows, window] += dot_nt(do_t[rows], prob_low)
        for j, ctx in enumerate((ctx_a, ctx_b, ctx_c, ctx_d)):

            @pl.when(i // (pl.num_programs(0) // 4) == jnp.bitwise_xor(me[0], j))
            def _():
                ctx[...] = jnp.concatenate(contexts, axis=0)

    for far in range(SEQ_MAX // QB + 1):
        pl.when(reach == far)(partial(run, far + 1))

    @pl.when(i == pl.num_programs(0) - 1)
    def _():
        kv[:width] = rope_t(dk_t[...], cosine[...], -sine[...]).astype(BF16)
        kv[width:] = dv_t[...].astype(BF16)


def attention(low_block, me, qkv, d_ctx, begin, cosine, sine, deps=()):
    width, total = d_ctx.shape
    heads = width // HEAD_DIM

    part = total // QB // 4

    def column(rows):
        return pl.BlockSpec((rows, QB), lambda i, m, r: (0, i))

    def whole(rows):
        return pl.BlockSpec((rows, total), lambda i, m, r: (0, 0))

    shards = [
        pl.BlockSpec(
            (width, QB),
            lambda i, m, r, j=j: (0, jnp.clip(i - jnp.bitwise_xor(r[0], j) * part, 0, part - 1)),
        )
        for j in range(4)
    ]

    return pl.pallas_call(
        waiting(attention_kernel, 2, 5, len(deps)),
        grid_spec=pltpu.PrefetchScalarGridSpec(
            num_scalar_prefetch=2,
            grid=(total // QB,),
            in_specs=[
                column(3 * width),
                column(width),
                column(1),
                whole(HALF_ROT),
                whole(HALF_ROT),
            ]
            + [pl.BlockSpec(memory_space=pl.ANY)] * len(deps),
            out_specs=shards + [column(width), whole(2 * width)],
            scratch_shapes=[
                pltpu.VMEM((heads, total, HEAD_DIM), BF16),
                pltpu.VMEM((heads, total, HEAD_DIM), BF16),
                pltpu.VMEM((width, total), BF16),
                pltpu.VMEM((width, total), BF16),
                pltpu.VMEM((width, total), F32),
                pltpu.VMEM((width, total), F32),
            ],
        ),
        out_shape=[jax.ShapeDtypeStruct((width, total // 4), BF16)] * 4
        + [
            jax.ShapeDtypeStruct((width, total), BF16),
            jax.ShapeDtypeStruct((2 * width, total), BF16),
        ],
        compiler_params=params(),
        cost_estimate=cost(46),
        name="attention",
    )(low_block, me, qkv, d_ctx, begin, cosine, sine, *deps)


def finish_kernel(last, me, *refs):
    ctx_a, ctx_b, dq, kv, tok_a, tok_b, g_a, g_b, normed, d_mlp, wat = refs[:11]
    if last:
        sums_in, total_in, dn_a, dn_b, sums, weight_g, total_g = refs[11:]
    else:
        dn_a, dn_b, sums, total_g = refs[11:]

    @pl.when(pl.program_id(0) == 0)
    def _():
        sums[...] = sums_in[...] if last else jnp.zeros_like(sums)
        total_g[...] = total_in[...] if last else jnp.zeros_like(total_g)

    own = dq.shape[0]
    n = normed[...]
    total = dot_nn(dq[...].T, wat[:own]) + dot_nn(kv[...].T, wat[own : 3 * own])
    total_g[:own] += dot_nn(dq[...], n)
    total_g[own : 3 * own] += dot_nn(kv[...], n)
    total_g[3 * own :] += dot_nn(of_list([ctx_a, ctx_b]), of_list([g_a, g_b]))
    total = total + d_mlp[...].astype(F32)
    unit, _ = unit_of(of_list([tok_a, tok_b]))
    sums[0:1] += jnp.sum(total * unit, axis=0, keepdims=True)
    sums[1:2] += jnp.sum(total, axis=0, keepdims=True)
    put_list([dn_a, dn_b], total.astype(BF16))
    if last:

        @pl.when(pl.program_id(0) == pl.num_programs(0) - 1)
        def _():
            weight_g[...] = total_g[...].T


def finish(me, ctxs, dq, kv, toks, grads, normed, d_mlp, wat, first, sofar=(), deps=(), block=384):
    shard, width = toks[0].shape
    sub = shard // block
    place = placing(first, sub)
    last = len(sofar) > 0

    def column(rows):
        return pl.BlockSpec((rows, block), lambda b, m: (0, place(b, m)))

    context = [
        pl.BlockSpec((width // 4, block), lambda b, m, k=k: (0, jnp.clip(b - k * sub, 0, sub - 1)))
        for k in range(2)
    ]
    two = list_specs(block, width, sub, 2)
    row = pl.BlockSpec((block, width), lambda b, m: (b, 0))
    square = pl.BlockSpec((width, width), lambda b, m: (0, 0))
    sums = pl.BlockSpec((8, width), lambda b, m: (0, 0))
    return pl.pallas_call(
        waiting(partial(finish_kernel, last), 1, 11 + len(sofar), len(deps)),
        grid_spec=pltpu.PrefetchScalarGridSpec(
            num_scalar_prefetch=1,
            grid=(2 * sub,),
            in_specs=context
            + [column(width // 4), column(width // 2)]
            + two
            + two
            + [row, row, square]
            + ([sums, square] if last else [])
            + [pl.BlockSpec(memory_space=pl.ANY)] * len(deps),
            out_specs=two + [sums, square],
            scratch_shapes=[pltpu.VMEM((width, width), F32)] if last else [],
        ),
        out_shape=[jax.ShapeDtypeStruct((shard, width), BF16)] * 2
        + [jax.ShapeDtypeStruct((8, width), F32), jax.ShapeDtypeStruct((width, width), F32)],
        compiler_params=params(),
        cost_estimate=cost(10),
        name="finish",
    )(me, *ctxs, dq, kv, *toks, *grads, normed, d_mlp, wat, *sofar, *deps)


def input_gradient_kernel(tok, cotangent, dn_a, dn_b, dn_c, gain, out):
    share = dn_a[...].astype(F32) + dn_b[...].astype(F32) + dn_c[...].astype(F32)
    unit, inv_std = unit_of(tok[...])
    unit_grad = share * gain[...]
    plain_mean = jnp.mean(unit_grad, axis=1, keepdims=True)
    cross_mean = jnp.mean(unit_grad * unit, axis=1, keepdims=True)
    out[...] = (
        cotangent[...].astype(F32) + inv_std * (unit_grad - plain_mean - unit * cross_mean)
    ).astype(BF16)


def input_gradient(tok, cotangent, dns, gain, deps=(), block=256):
    shard, width = tok.shape
    row = pl.BlockSpec((block, width), lambda b: (b, 0))
    return pl.pallas_call(
        waiting(input_gradient_kernel, 0, 6, len(deps)),
        grid=(shard // block,),
        in_specs=[row] * 5
        + [pl.BlockSpec((1, width), lambda b: (0, 0))]
        + [pl.BlockSpec(memory_space=pl.ANY)] * len(deps),
        out_specs=row,
        out_shape=jax.ShapeDtypeStruct((shard, width), BF16),
        compiler_params=params(),
        cost_estimate=cost(5),
        name="input_gradient",
    )(tok, cotangent, *dns, gain, *deps)


def mix_kernel(tok, mlp_a, mlp_b, mlp_c, *rest):
    ctxs, weights, mixed = rest[:4], rest[4:8], rest[8]
    total = tok[...].astype(F32) + mlp_a[...].astype(F32)
    total = total + (mlp_b[...].astype(F32) + mlp_c[...].astype(F32))
    for ctx, weight in zip(ctxs, weights):
        total = total + dot_nn(ctx[...].T, weight[...])
    mixed[...] = total.astype(BF16)


def mix(tok, mlps, ctxs, chip_got, last_ctx, weights, deps=(), block=384):
    shard, width = tok.shape
    own = width // 4
    row = pl.BlockSpec((block, width), lambda b: (b, 0))
    return pl.pallas_call(
        waiting(mix_kernel, 0, 12, len(deps)),
        grid=(shard // block,),
        in_specs=[row] * 4
        + [pl.BlockSpec((own, block), lambda b: (0, b))] * 2
        + [pl.BlockSpec((own, block), lambda b: (shard // own, b))]
        + [pl.BlockSpec((own, block), lambda b: (0, b))]
        + [pl.BlockSpec((own, width), lambda b: (0, 0))] * 4
        + [pl.BlockSpec(memory_space=pl.ANY)] * len(deps),
        out_specs=row,
        out_shape=jax.ShapeDtypeStruct((shard, width), BF16),
        compiler_params=params(),
        cost_estimate=cost(5),
        name="mix",
    )(tok, *mlps, *ctxs, chip_got, last_ctx, *weights, *deps)


def together(*values, deps=()):
    def nothing(*refs):
        pass

    anywhere = pl.BlockSpec(memory_space=pl.ANY)
    return pl.pallas_call(
        nothing,
        in_specs=[anywhere] * (len(values) + len(deps)),
        out_specs=[anywhere] * len(values),
        out_shape=[jax.ShapeDtypeStruct(value.shape, value.dtype) for value in values],
        input_output_aliases={k: k for k in range(len(values))},
        cost_estimate=cost(1),
        name="together",
    )(*values, *deps)


def after(value, *deps):
    return together(value, deps=deps)[0]


def swap(value, axis, size, bit):
    return lax.ppermute(value, axis, [(i, i ^ bit) for i in range(size)])


def bits_of(size):
    out, bit = [], 1
    while bit < size:
        out.insert(0, bit)
        bit *= 2
    return out


class Gather:
    def __init__(self, shard, size, me):
        self.held, self.done, self.size, self.me = shard, [], size, me

    def send(self, bit):
        self.bit = bit
        self.theirs = swap(self.held, "dp", self.size, bit)

    def whole(self):
        return self.held.reshape(-1, self.held.shape[-1])


def merge_kernel(second, *refs):
    count = len(refs) // 3
    for k in range(count):
        held, theirs, out = refs[2 * k], refs[2 * k + 1], refs[2 * count + k]
        for high in range(held.shape[0]):
            out[high, second[k]] = held[high]
            out[high, 1 - second[k]] = theirs[high]


def merge(gathers, deps=()):
    second, parts, shapes = [], [], []
    for gather in gathers:
        second.append(((gather.me & gather.bit) != 0).astype(jnp.int32))
        high = 2 ** sum(1 for other in gather.done if other > gather.bit)
        gather.done.append(gather.bit)
        width = gather.held.shape[-1]
        one = (high, gather.held.size // (high * width), width)
        parts += [gather.held.reshape(one), gather.theirs.reshape(one)]
        shapes.append(jax.ShapeDtypeStruct((one[0], 2, *one[1:]), gather.held.dtype))

    def whole(shape):
        return pl.BlockSpec(shape, lambda b, m: (0,) * len(shape))

    outs = pl.pallas_call(
        waiting(merge_kernel, 1, len(parts), len(deps)),
        grid_spec=pltpu.PrefetchScalarGridSpec(
            num_scalar_prefetch=1,
            grid=(1,),
            in_specs=[whole(part.shape) for part in parts]
            + [pl.BlockSpec(memory_space=pl.ANY)] * len(deps),
            out_specs=[whole(shape.shape) for shape in shapes],
        ),
        out_shape=shapes,
        compiler_params=params(),
        cost_estimate=cost(2),
        name="merge",
    )(jnp.stack(second), *parts, *deps)
    for gather, out in zip(gathers, outs):
        gather.held = out


class Scatter:
    def __init__(self, whole, size, me):
        rows, width = whole.shape
        self.left, self.size, self.me = bits_of(size), size, me
        self.held = whole.reshape((2,) * len(self.left) + (rows // size, width))

    def send(self, bit, deps=()):
        axis = self.left.index(bit)
        self.left.remove(bit)
        mine = ((self.me & bit) != 0).astype(jnp.int32)
        self.keep = lax.dynamic_index_in_dim(self.held, mine, axis, keepdims=False)
        away = lax.dynamic_index_in_dim(self.held, 1 - mine, axis, keepdims=False)
        self.away = away.astype(BF16)
        if deps:
            self.away = after(self.away, *deps)
        self.theirs = swap(self.away, "dp", self.size, bit)

    def take(self):
        self.held = self.keep.astype(F32) + self.theirs.astype(F32)

    def send_last(self):
        high, low = self.left
        quarters = self.held.reshape(4, *self.held.shape[2:])
        place = (self.me // low) % 4
        self.keep = lax.dynamic_index_in_dim(quarters, place, 0, keepdims=False).astype(F32)
        self.aways = [
            lax.dynamic_index_in_dim(quarters, place ^ k, 0, keepdims=False).astype(BF16)
            for k in range(1, 4)
        ]
        self.parts = [swap(self.aways[k - 1], "dp", self.size, k * low) for k in range(1, 4)]

    def take_last(self):
        one, two, three = [part.astype(F32) for part in self.parts]
        self.held = (self.keep + one) + (two + three)


def sum_over(value, axis, size, bits):
    if len(bits) == 1:
        return value + swap(value, axis, size, bits[0])
    far, near = bits
    parts = together(*[swap(value, axis, size, bit) for bit in (near, far, far + near)])
    return (value + parts[0]) + (parts[1] + parts[2])


def tables(lengths, count):
    doc_ends = jnp.cumsum(lengths)
    places = jnp.arange(count, dtype=jnp.int32)
    after_end = places[:, None] >= doc_ends[None, :]
    begins = jnp.max(jnp.where(after_end, doc_ends[None, :], 0), axis=1)
    offset_f = (places - begins).astype(F32)
    frequency = jnp.exp(
        -(2.0 * jnp.arange(HALF_ROT, dtype=F32) / ROT_DIM) * math.log(10000.0)
    )
    angle = frequency[:, None] * offset_f[None, :]
    low_block = begins.reshape(count // QB, QB)[:, 0] // QB
    return begins[None, :], low_block, jnp.cos(angle), jnp.sin(angle)


def body(
    n_dp, n_row, tokens, ln_gain, ln_bias, w_query, w_key, w_value, w_out, w_up, w_down, doc_lengths, cotangent
):
    shard, width = tokens.shape
    total = shard * n_row
    own = width // n_row
    hid = w_up.shape[1]
    dp_me = lax.axis_index("dp")
    row_me = lax.axis_index("row").astype(jnp.int32)
    me = row_me.reshape(1)
    bits = bits_of(n_dp)
    to_core = partial(swap, axis="row", size=n_row, bit=1)
    to_chip = partial(swap, axis="row", size=n_row, bit=2)
    to_both = partial(swap, axis="row", size=n_row, bit=3)

    tok = [tokens, to_core(tokens), to_chip(tokens)]
    grad = [cotangent, to_core(cotangent)]
    up = Gather(w_up, n_dp, dp_me)
    down = Gather(w_down.T, n_dp, dp_me)
    orders = list(zip(bits, bits[-1:] + bits[:-1]))
    attn_shard = jnp.concatenate([w_query, w_key, w_value, w_out.T], axis=1)
    attn = Gather(attn_shard, n_dp, dp_me)
    for k, (first, second) in enumerate(orders):
        up.send(first)
        down.send(second)
        if k == 0:
            for bit in bits[:1:-1]:
                attn.send(bit)
                attn_ready = attn.theirs
                merge([attn])
        merge([up, down], (attn_ready, tok[2]) if k + 2 == len(orders) else ())
    grad.append(to_chip(cotangent))
    begin, low_block, cosine, sine = tables(doc_lengths[0], total)
    gain, bias = ln_gain[None, :], ln_bias[None, :]

    up_w, down_w = up.whole(), down.whole()
    quarter = attn.whole()
    quarters = [swap(quarter, "dp", n_dp, bit) for bit in (bits[1], bits[0], bits[0] + bits[1])]
    near_n, *near_mlp, near_dm, ffn_g = feed_forward(
        tok[:2], grad[:2], gain, bias, up_w, down_w, (), (quarter, cosine, sine, begin)
    )
    tok.append(to_core(after(tok[2], near_dm, *quarters)))
    grad[2] = after(grad[2], near_dm, *quarters)
    grad.append(to_core(grad[2]))
    wat, own_out = assemble((dp_me // bits[1]).astype(jnp.int32).reshape(1), [quarter, *quarters])
    far_n, *far_mlp, far_dm, ffn_g = feed_forward(
        tok[2:], grad[2:], gain, bias, up_w, down_w, (ffn_g,), (wat,)
    )
    ffn_wg = lax.psum_scatter(ffn_g, "dp", scatter_dimension=0, tiled=True)
    far_mlp_core = to_core(far_mlp[1])
    near_mlp_core = to_core(near_mlp[1])

    qkv, d_ctx = project(me, [near_n, far_n], grad, wat, cosine, sine)
    far_mlp_core = after(far_mlp_core, qkv)
    mlp_both = (far_mlp[0].astype(F32) + far_mlp_core.astype(F32)).astype(BF16)
    mlp_chip = to_chip(mlp_both)
    out_w = [own_out]
    out_w += [to_core(out_w[0]), to_chip(out_w[0]), to_both(out_w[0])]

    *ctx, dq, kv = attention(
        low_block, me, qkv, d_ctx, begin, cosine, sine, (mlp_both,)
    )

    ctxs = [ctx[0], to_core(ctx[1])]
    far_dn, far_dn_b, *sofar = finish(
        me, ctx[2:], dq, kv, tok[2:], grad[2:], far_n, far_dm, wat, 2, (), (mlp_chip, *out_w[1:])
    )
    theirs = to_core(far_dn_b)
    both = (far_dn.astype(F32) + theirs.astype(F32)).astype(BF16)
    away = jnp.concatenate([both, ctx[2], ctx[3]], axis=0)
    chip_got = to_chip(away)
    near_dn, near_dn_b, sums, attn_g = finish(
        me, ctx[:2], dq, kv, tok[:2], grad[:2], near_n, near_dm, wat, 0, sofar,
        (away, ffn_wg),
    )
    dn_core = to_core(near_dn_b)
    attn_sum = Scatter(attn_g, n_dp, dp_me)
    for bit in bits[:2:-1]:
        attn_sum.send(bit)
        attn_sum.take()
        sums = sum_over(sums, "dp", n_dp, [bit])
    attn_sum.send(bits[2])
    sums = sum_over(after(sums, attn_sum.away), "dp", n_dp, bits[:2])
    attn_sum.theirs = after(attn_sum.theirs, sums)
    attn_sum.take()
    attn_sum.send_last()
    sums = sum_over(after(sums, *attn_sum.aways), "dp", n_dp, bits[2:3])
    sums = sum_over(sums, "row", n_row, [2, 1])
    last_ctx = to_core(chip_got[shard + own :])
    mixed = mix(
        tokens, [near_mlp[0], near_mlp_core, mlp_chip], ctxs, chip_got, last_ctx, out_w, attn_sum.aways
    )
    input_grad = input_gradient(tokens, cotangent, [near_dn, dn_core, chip_got], gain, (mixed,))
    attn_sum.parts[0] = after(attn_sum.parts[0], input_grad)
    attn_sum.take_last()

    attn_wg, ffn_wg = attn_sum.held, ffn_wg.astype(F32)
    return (
        mixed,
        input_grad,
        sums[0],
        sums[1],
        attn_wg[:, :own],
        attn_wg[:, own : 2 * own],
        attn_wg[:, 2 * own : 3 * own],
        attn_wg[:, 3 * own :].T,
        ffn_wg[:, :hid],
        ffn_wg[:, hid:].T,
    )


def solution(mesh):
    in_specs = (
        P(("dp", "row"), None),
        P(),
        P(),
        P("dp", "row"),
        P("dp", "row"),
        P("dp", "row"),
        P("row", "dp"),
        P("dp", "row"),
        P("row", "dp"),
        P("dp", None),
        P(("dp", "row"), None),
    )
    out_specs = (
        P(("dp", "row"), None),
        P(("dp", "row"), None),
        P(),
        P(),
        P("dp", "row"),
        P("dp", "row"),
        P("dp", "row"),
        P("row", "dp"),
        P("dp", "row"),
        P("row", "dp"),
    )
    sizes = (mesh.shape["dp"], mesh.shape["row"])
    return jax.shard_map(
        partial(body, *sizes), mesh=mesh, in_specs=in_specs, out_specs=out_specs, check_vma=False
    )
```

```python
from functools import partial
import math

import jax
import jax.numpy as jnp
from jax import lax
from jax.experimental import pallas as pl
from jax.experimental.pallas import tpu as pltpu
from jax.sharding import PartitionSpec as P

HEAD_DIM = 64
ROT_DIM = 16
HALF_ROT = ROT_DIM // 2
SEQ_MAX = 1024
QB = 256
EPS = 1e-05
MASKED = -1000000000.0
MIB = 1024 * 1024
F32 = jnp.float32
BF16 = jnp.bfloat16


def dot_nn(a, b):
    return lax.dot_general(a, b, (((1,), (0,)), ((), ())), preferred_element_type=F32)


def dot_nt(a, b):
    return lax.dot_general(a, b, (((1,), (1,)), ((), ())), preferred_element_type=F32)


def dot_tn(a, b):
    return lax.dot_general(a, b, (((0,), (0,)), ((), ())), preferred_element_type=F32)


def unit_of(rows):
    inputs = rows.astype(F32)
    average = jnp.mean(inputs, axis=1, keepdims=True)
    centered = inputs - average
    spread_sq = jnp.mean(centered * centered, axis=1, keepdims=True)
    inv_std = lax.rsqrt(spread_sq + EPS)
    return centered * inv_std, inv_std


def rope_t(field, cosine, sine):
    heads = field.shape[0] // HEAD_DIM
    pieces = []
    for h in range(heads):
        one = field[h * HEAD_DIM : (h + 1) * HEAD_DIM]
        first, second = one[:HALF_ROT], one[HALF_ROT:ROT_DIM]
        pieces += [
            first * cosine - second * sine,
            second * cosine + first * sine,
            one[ROT_DIM:],
        ]
    return jnp.concatenate(pieces, axis=0)


def params(limit=56):
    return pltpu.CompilerParams(vmem_limit_bytes=limit * MIB)


def placing(first, sub):
    def place(b, me_ref):
        return jnp.bitwise_xor(me_ref[0], first + b // sub) * sub + b % sub

    return place


def list_specs(block, width, sub, count):
    return [
        pl.BlockSpec((block, width), lambda b, m, k=k: (jnp.clip(b - k * sub, 0, sub - 1), 0))
        for k in range(count)
    ]


def waiting(kernel, scalars, operands, deps):
    ahead = scalars + operands

    def run(*refs):
        kernel(*refs[:ahead], *refs[ahead + deps :])

    return run


def of_list(refs):
    part = pl.num_programs(0) // len(refs)
    out = refs[0][...]
    for k in range(1, len(refs)):
        out = jnp.where(pl.program_id(0) >= k * part, refs[k][...], out)
    return out


def put_list(refs, value):
    part = pl.num_programs(0) // len(refs)
    for k, ref in enumerate(refs):

        @pl.when(pl.program_id(0) // part == k)
        def _():
            ref[...] = value


def cost(micros):
    return pl.CostEstimate(flops=int(micros * 9.612e+07), bytes_accessed=1, transcendentals=0)


def ffn_kernel(tok_a, tok_b, g_a, g_b, gain, bias, w_up, w_down_t, *rest):
    hid = w_up.shape[1]
    last = len(rest) > 5
    if last:
        sofar, normed, mlp_a, mlp_b, d_normed, weight_out, weight_g = rest
    else:
        normed, mlp_a, mlp_b, d_normed, weight_g = rest

    @pl.when(pl.program_id(0) == 0)
    def _():
        weight_g[...] = sofar[...] if last else jnp.zeros_like(weight_g)

    unit, _ = unit_of(of_list([tok_a, tok_b]))
    n, g = (unit * gain[...] + bias[...]).astype(BF16), of_list([g_a, g_b])
    normed[...] = n
    up_pre = dot_nn(n, w_up[...])
    d_hidden = dot_nn(g, w_down_t[...])
    cdf = 0.5 * (1.0 + lax.erf(up_pre * (2.0**-0.5)))
    pdf = jnp.exp(-0.5 * up_pre * up_pre) * ((2.0 * math.pi) ** -0.5)
    hidden = (up_pre * cdf).astype(BF16)
    d_up = (d_hidden * (cdf + up_pre * pdf)).astype(BF16)
    branch = dot_nt(hidden, w_down_t[...]).astype(BF16)
    d_normed[...] = dot_nt(d_up, w_up[...]).astype(BF16)
    weight_g[:, :hid] += dot_tn(n, d_up)
    weight_g[:, hid:] += dot_tn(g, hidden)
    put_list([mlp_a, mlp_b], branch)
    if last:

        @pl.when(pl.program_id(0) == pl.num_programs(0) - 1)
        def _():
            weight_out[...] = weight_g[...].astype(BF16)


def feed_forward(toks, grads, gain, bias, w_up, w_down_t, sofar, deps=(), block=768):
    shard, width = grads[0].shape
    count = 2 * shard
    hid = w_up.shape[1]
    sub = shard // block
    row = pl.BlockSpec((block, width), lambda b: (b, 0))
    half = [
        pl.BlockSpec((block, width), lambda b, k=k: (jnp.clip(b - k * sub, 0, sub - 1), 0))
        for k in range(2)
    ]
    one = pl.BlockSpec((1, width), lambda b: (0, 0))
    square = pl.BlockSpec((width, hid), lambda b: (0, 0))
    double = pl.BlockSpec((width, 2 * hid), lambda b: (0, 0))
    return pl.pallas_call(
        waiting(ffn_kernel, 0, 8 + len(sofar), len(deps)),
        grid=(2 * sub,),
        in_specs=half + half + [one, one, square, square] + [double] * len(sofar) + [pl.BlockSpec(memory_space=pl.ANY)] * len(deps),
        out_specs=[row] + half + [row, double],
        out_shape=[
            jax.ShapeDtypeStruct((count, width), BF16),
            jax.ShapeDtypeStruct((shard, width), BF16),
            jax.ShapeDtypeStruct((shard, width), BF16),
            jax.ShapeDtypeStruct((count, width), BF16),
            jax.ShapeDtypeStruct((width, 2 * hid), BF16 if sofar else F32),
        ],
        scratch_shapes=[pltpu.VMEM((width, 2 * hid), F32)] * len(sofar),
        compiler_params=params(),
        cost_estimate=cost(8),
        name="feed_forward",
    )(*toks, *grads, gain, bias, w_up, w_down_t, *sofar, *deps)


def assemble_kernel(me, part_a, part_b, part_c, part_d, out, last, whole):
    rows = part_a.shape[0]
    for k, part in enumerate((part_a, part_b, part_c, part_d)):
        whole[pl.ds(pl.multiple_of(jnp.bitwise_xor(me[0], k) * rows, rows), rows)] = part[...]
    turned = whole[...].T
    out[...] = turned
    last[...] = turned[3 * last.shape[0] :]


def assemble(me, parts):
    rows, width = parts[0].shape
    return pl.pallas_call(
        assemble_kernel,
        grid_spec=pltpu.PrefetchScalarGridSpec(
            num_scalar_prefetch=1,
            grid=(1,),
            in_specs=[pl.BlockSpec((rows, width), lambda b, m: (0, 0))] * 4,
            out_specs=[
                pl.BlockSpec((width, 4 * rows), lambda b, m: (0, 0)),
                pl.BlockSpec((width // 4, 4 * rows), lambda b, m: (0, 0)),
            ],
            scratch_shapes=[pltpu.VMEM((4 * rows, width), BF16)],
        ),
        out_shape=[
            jax.ShapeDtypeStruct((width, 4 * rows), BF16),
            jax.ShapeDtypeStruct((width // 4, 4 * rows), BF16),
        ],
        compiler_params=params(),
        cost_estimate=cost(3),
        name="assemble",
    )(me, *parts)


def project_kernel(me, n_a, n_b, g_a, g_b, g_c, g_d, wat, cosine, sine, qkv, d_ctx):
    low = of_list([n_a, n_b])
    width = d_ctx.shape[0]
    out = dot_nt(wat[: 3 * width], low)
    d_ctx[...] = dot_nt(wat[3 * width :], of_list([g_a, g_b, g_c, g_d])).astype(BF16)
    cos_b, sin_b = cosine[...], sine[...]
    scale = HEAD_DIM ** (-0.5)
    qkv[:width] = (rope_t(out[:width], cos_b, sin_b) * scale).astype(BF16)
    qkv[width : 2 * width] = rope_t(out[width : 2 * width], cos_b, sin_b).astype(BF16)
    qkv[2 * width :] = out[2 * width :].astype(BF16)


def project(me, normeds, grads, wat, cosine, sine, deps=(), block=768):
    shard, width = grads[0].shape
    total = cosine.shape[1]
    sub = shard // block
    own = width // 4
    place = placing(0, sub)
    table = pl.BlockSpec((HALF_ROT, block), lambda b, m: (0, place(b, m)))
    return pl.pallas_call(
        waiting(project_kernel, 1, 9, len(deps)),
        grid_spec=pltpu.PrefetchScalarGridSpec(
            num_scalar_prefetch=1,
            grid=(4 * sub,),
            in_specs=list_specs(block, width, 2 * sub, 2)
            + list_specs(block, width, sub, 4)
            + [pl.BlockSpec((4 * own, width), lambda b, m: (0, 0)), table, table]
            + [pl.BlockSpec(memory_space=pl.ANY)] * len(deps),
            out_specs=[
                pl.BlockSpec((3 * own, block), lambda b, m: (0, place(b, m))),
                pl.BlockSpec((own, block), lambda b, m: (0, place(b, m))),
            ],
        ),
        out_shape=[
            jax.ShapeDtypeStruct((3 * own, total), BF16),
            jax.ShapeDtypeStruct((own, total), BF16),
        ],
        compiler_params=params(),
        cost_estimate=cost(11),
        name="project",
    )(me, *normeds, *grads, wat, cosine, sine, *deps)


def attention_kernel(low_block, me, qkv, d_ctx, begin, cosine, sine, ctx_a, ctx_b, ctx_c, ctx_d, dq, kv, k_rows, v_rows, k_t, v_t, dk_t, dv_t):
    i = pl.program_id(0)
    width = d_ctx.shape[0]
    heads = width // HEAD_DIM
    here = pl.multiple_of(i * QB, QB)
    q_t = qkv[:width]
    k_here = qkv[width : 2 * width]
    v_here = qkv[2 * width :]
    k_t[:, pl.ds(here, QB)] = k_here
    v_t[:, pl.ds(here, QB)] = v_here
    k_nat = k_here.T
    v_nat = v_here.T
    for h in range(heads):
        cols = slice(h * HEAD_DIM, (h + 1) * HEAD_DIM)
        k_rows[h, pl.ds(here, QB), :] = k_nat[:, cols]
        v_rows[h, pl.ds(here, QB), :] = v_nat[:, cols]
    dk_t[:, pl.ds(here, QB)] = jnp.zeros((width, QB), F32)
    dv_t[:, pl.ds(here, QB)] = jnp.zeros((width, QB), F32)
    base = low_block[i]
    start = pl.multiple_of(base * QB, QB)
    reach = i - base
    first_key = begin[...] - start
    last_key = lax.broadcasted_iota(jnp.int32, (1, QB), 1) + (here - start)
    do_t = d_ctx[...]
    cos_here = cosine[:, pl.ds(here, QB)]
    sin_here = sine[:, pl.ds(here, QB)]
    scale = HEAD_DIM ** (-0.5)

    def run(blocks):
        span = blocks * QB
        key = lax.broadcasted_iota(jnp.int32, (span, QB), 0)
        allowed = (key >= first_key) & (key <= last_key)
        window = pl.ds(start, span)
        contexts = []
        head_rows = [slice(h * HEAD_DIM, (h + 1) * HEAD_DIM) for h in range(heads)]
        kept = []
        all_scores = [dot_nn(k_rows[h, window, :], q_t[rows]) for h, rows in enumerate(head_rows)]
        all_d_prob = [dot_nn(v_rows[h, window, :], do_t[rows]) for h, rows in enumerate(head_rows)]
        for h, rows in enumerate(head_rows):
            scores = jnp.where(allowed, all_scores[h], MASKED)
            highest = jnp.max(scores, axis=0, keepdims=True)
            expo = jnp.exp(scores - highest)
            prob = expo * (1.0 / jnp.sum(expo, axis=0, keepdims=True))
            prob_low = prob.astype(BF16)
            context = dot_nn(v_t[rows, window], prob_low)
            kept.append((prob, prob_low, context))
        for h, rows in enumerate(head_rows):
            prob, prob_low, context = kept[h]
            delta = jnp.sum(do_t[rows].astype(F32) * context, axis=0, keepdims=True)
            d_scores = (prob * (all_d_prob[h] - delta)).astype(BF16)
            dq_h = dot_nn(k_t[rows, window], d_scores) * scale
            dq[rows] = rope_t(dq_h, cos_here, -sin_here).astype(BF16)
            contexts.append(context.astype(BF16))
            dk_t[rows, window] += dot_nt(q_t[rows], d_scores)
            dv_t[rows, window] += dot_nt(do_t[rows], prob_low)
        for j, ctx in enumerate((ctx_a, ctx_b, ctx_c, ctx_d)):

            @pl.when(i // (pl.num_programs(0) // 4) == jnp.bitwise_xor(me[0], j))
            def _():
                ctx[...] = jnp.concatenate(contexts, axis=0)

    for far in range(SEQ_MAX // QB + 1):
        pl.when(reach == far)(partial(run, far + 1))

    @pl.when(i == pl.num_programs(0) - 1)
    def _():
        kv[:width] = rope_t(dk_t[...], cosine[...], -sine[...]).astype(BF16)
        kv[width:] = dv_t[...].astype(BF16)


def attention(low_block, me, qkv, d_ctx, begin, cosine, sine, deps=()):
    width, total = d_ctx.shape
    heads = width // HEAD_DIM

    part = total // QB // 4

    def column(rows):
        return pl.BlockSpec((rows, QB), lambda i, m, r: (0, i))

    def whole(rows):
        return pl.BlockSpec((rows, total), lambda i, m, r: (0, 0))

    shards = [
        pl.BlockSpec(
            (width, QB),
            lambda i, m, r, j=j: (0, jnp.clip(i - jnp.bitwise_xor(r[0], j) * part, 0, part - 1)),
        )
        for j in range(4)
    ]

    return pl.pallas_call(
        waiting(attention_kernel, 2, 5, len(deps)),
        grid_spec=pltpu.PrefetchScalarGridSpec(
            num_scalar_prefetch=2,
            grid=(total // QB,),
            in_specs=[
                column(3 * width),
                column(width),
                column(1),
                whole(HALF_ROT),
                whole(HALF_ROT),
            ]
            + [pl.BlockSpec(memory_space=pl.ANY)] * len(deps),
            out_specs=shards + [column(width), whole(2 * width)],
            scratch_shapes=[
                pltpu.VMEM((heads, total, HEAD_DIM), BF16),
                pltpu.VMEM((heads, total, HEAD_DIM), BF16),
                pltpu.VMEM((width, total), BF16),
                pltpu.VMEM((width, total), BF16),
                pltpu.VMEM((width, total), F32),
                pltpu.VMEM((width, total), F32),
            ],
        ),
        out_shape=[jax.ShapeDtypeStruct((width, total // 4), BF16)] * 4
        + [
            jax.ShapeDtypeStruct((width, total), BF16),
            jax.ShapeDtypeStruct((2 * width, total), BF16),
        ],
        compiler_params=params(),
        cost_estimate=cost(46),
        name="attention",
    )(low_block, me, qkv, d_ctx, begin, cosine, sine, *deps)


def finish_kernel(last, me, *refs):
    ctx_a, ctx_b, dq, kv, tok_a, tok_b, g_a, g_b, normed, d_mlp, wat = refs[:11]
    if last:
        sums_in, total_in, dn_a, dn_b, sums, weight_g, total_g = refs[11:]
    else:
        dn_a, dn_b, sums, total_g = refs[11:]

    @pl.when(pl.program_id(0) == 0)
    def _():
        sums[...] = sums_in[...] if last else jnp.zeros_like(sums)
        total_g[...] = total_in[...] if last else jnp.zeros_like(total_g)

    own = dq.shape[0]
    n = normed[...]
    total = dot_nn(dq[...].T, wat[:own]) + dot_nn(kv[...].T, wat[own : 3 * own])
    total_g[:own] += dot_nn(dq[...], n)
    total_g[own : 3 * own] += dot_nn(kv[...], n)
    total_g[3 * own :] += dot_nn(of_list([ctx_a, ctx_b]), of_list([g_a, g_b]))
    total = total + d_mlp[...].astype(F32)
    unit, _ = unit_of(of_list([tok_a, tok_b]))
    sums[0:1] += jnp.sum(total * unit, axis=0, keepdims=True)
    sums[1:2] += jnp.sum(total, axis=0, keepdims=True)
    put_list([dn_a, dn_b], total.astype(BF16))
    if last:

        @pl.when(pl.program_id(0) == pl.num_programs(0) - 1)
        def _():
            weight_g[...] = total_g[...].T


def finish(me, ctxs, dq, kv, toks, grads, normed, d_mlp, wat, first, sofar=(), deps=(), block=384):
    shard, width = toks[0].shape
    sub = shard // block
    place = placing(first, sub)
    last = len(sofar) > 0

    def column(rows):
        return pl.BlockSpec((rows, block), lambda b, m: (0, place(b, m)))

    context = [
        pl.BlockSpec((width // 4, block), lambda b, m, k=k: (0, jnp.clip(b - k * sub, 0, sub - 1)))
        for k in range(2)
    ]
    two = list_specs(block, width, sub, 2)
    row = pl.BlockSpec((block, width), lambda b, m: (b, 0))
    square = pl.BlockSpec((width, width), lambda b, m: (0, 0))
    sums = pl.BlockSpec((8, width), lambda b, m: (0, 0))
    return pl.pallas_call(
        waiting(partial(finish_kernel, last), 1, 11 + len(sofar), len(deps)),
        grid_spec=pltpu.PrefetchScalarGridSpec(
            num_scalar_prefetch=1,
            grid=(2 * sub,),
            in_specs=context
            + [column(width // 4), column(width // 2)]
            + two
            + two
            + [row, row, square]
            + ([sums, square] if last else [])
            + [pl.BlockSpec(memory_space=pl.ANY)] * len(deps),
            out_specs=two + [sums, square],
            scratch_shapes=[pltpu.VMEM((width, width), F32)] if last else [],
        ),
        out_shape=[jax.ShapeDtypeStruct((shard, width), BF16)] * 2
        + [jax.ShapeDtypeStruct((8, width), F32), jax.ShapeDtypeStruct((width, width), F32)],
        compiler_params=params(),
        cost_estimate=cost(10),
        name="finish",
    )(me, *ctxs, dq, kv, *toks, *grads, normed, d_mlp, wat, *sofar, *deps)


def output_kernel(tok, cotangent, gain, dn_a, dn_b, dn_c, mlp_a, mlp_b, mlp_c, *rest):
    ctxs, weights, (mixed, input_grad) = rest[:4], rest[4:8], rest[8:]
    inputs = tok[...].astype(F32)
    total = inputs + mlp_a[...].astype(F32)
    total = total + (mlp_b[...].astype(F32) + mlp_c[...].astype(F32))
    for ctx, weight in zip(ctxs, weights):
        total = total + dot_nn(ctx[...].T, weight[...])
    mixed[...] = total.astype(BF16)
    share = dn_a[...].astype(F32) + dn_b[...].astype(F32) + dn_c[...].astype(F32)
    unit, inv_std = unit_of(tok[...])
    unit_grad = share * gain[...]
    plain_mean = jnp.mean(unit_grad, axis=1, keepdims=True)
    cross_mean = jnp.mean(unit_grad * unit, axis=1, keepdims=True)
    input_grad[...] = (
        cotangent[...].astype(F32) + inv_std * (unit_grad - plain_mean - unit * cross_mean)
    ).astype(BF16)


def row_outputs(tok, cotangent, gain, dns, mlps, ctxs, chip_got, last_ctx, weights, deps=(), block=384):
    shard, width = tok.shape
    own = width // 4
    row = pl.BlockSpec((block, width), lambda b: (b, 0))
    column = pl.BlockSpec((own, block), lambda b: (0, b))
    return pl.pallas_call(
        waiting(output_kernel, 0, 17, len(deps)),
        grid=(shard // block,),
        in_specs=[row, row, pl.BlockSpec((1, width), lambda b: (0, 0))]
        + [row] * 6
        + [column, column, pl.BlockSpec((own, block), lambda b: (shard // own, b)), column]
        + [pl.BlockSpec((own, width), lambda b: (0, 0))] * 4
        + [pl.BlockSpec(memory_space=pl.ANY)] * len(deps),
        out_specs=[row, row],
        out_shape=[jax.ShapeDtypeStruct((shard, width), BF16)] * 2,
        compiler_params=params(),
        cost_estimate=cost(8),
        name="row_outputs",
    )(tok, cotangent, gain, *dns, *mlps, *ctxs, chip_got, last_ctx, *weights, *deps)


def together(*values, deps=()):
    def nothing(*refs):
        pass

    anywhere = pl.BlockSpec(memory_space=pl.ANY)
    return pl.pallas_call(
        nothing,
        in_specs=[anywhere] * (len(values) + len(deps)),
        out_specs=[anywhere] * len(values),
        out_shape=[jax.ShapeDtypeStruct(value.shape, value.dtype) for value in values],
        input_output_aliases={k: k for k in range(len(values))},
        cost_estimate=cost(1),
        name="together",
    )(*values, *deps)


def after(value, *deps):
    return together(value, deps=deps)[0]


def swap(value, axis, size, bit):
    return lax.ppermute(value, axis, [(i, i ^ bit) for i in range(size)])


def bits_of(size):
    out, bit = [], 1
    while bit < size:
        out.insert(0, bit)
        bit *= 2
    return out


class Gather:
    def __init__(self, shard, size, me):
        self.held, self.done, self.size, self.me = shard, [], size, me

    def send(self, bit):
        self.bit = bit
        self.theirs = swap(self.held, "dp", self.size, bit)

    def whole(self):
        return self.held.reshape(-1, self.held.shape[-1])


def merge_kernel(second, *refs):
    count = len(refs) // 3
    for k in range(count):
        held, theirs, out = refs[2 * k], refs[2 * k + 1], refs[2 * count + k]
        for high in range(held.shape[0]):
            out[high, second[k]] = held[high]
            out[high, 1 - second[k]] = theirs[high]


def merge(gathers, deps=()):
    second, parts, shapes = [], [], []
    for gather in gathers:
        second.append(((gather.me & gather.bit) != 0).astype(jnp.int32))
        high = 2 ** sum(1 for other in gather.done if other > gather.bit)
        gather.done.append(gather.bit)
        width = gather.held.shape[-1]
        one = (high, gather.held.size // (high * width), width)
        parts += [gather.held.reshape(one), gather.theirs.reshape(one)]
        shapes.append(jax.ShapeDtypeStruct((one[0], 2, *one[1:]), gather.held.dtype))

    def whole(shape):
        return pl.BlockSpec(shape, lambda b, m: (0,) * len(shape))

    outs = pl.pallas_call(
        waiting(merge_kernel, 1, len(parts), len(deps)),
        grid_spec=pltpu.PrefetchScalarGridSpec(
            num_scalar_prefetch=1,
            grid=(1,),
            in_specs=[whole(part.shape) for part in parts]
            + [pl.BlockSpec(memory_space=pl.ANY)] * len(deps),
            out_specs=[whole(shape.shape) for shape in shapes],
        ),
        out_shape=shapes,
        compiler_params=params(),
        cost_estimate=cost(2),
        name="merge",
    )(jnp.stack(second), *parts, *deps)
    for gather, out in zip(gathers, outs):
        gather.held = out


class Scatter:
    def __init__(self, whole, size, me):
        rows, width = whole.shape
        self.left, self.size, self.me = bits_of(size), size, me
        self.held = whole.reshape((2,) * len(self.left) + (rows // size, width))

    def send(self, bit, deps=()):
        axis = self.left.index(bit)
        self.left.remove(bit)
        mine = ((self.me & bit) != 0).astype(jnp.int32)
        self.keep = lax.dynamic_index_in_dim(self.held, mine, axis, keepdims=False)
        away = lax.dynamic_index_in_dim(self.held, 1 - mine, axis, keepdims=False)
        self.away = away.astype(BF16)
        if deps:
            self.away = after(self.away, *deps)
        self.theirs = swap(self.away, "dp", self.size, bit)

    def take(self):
        self.held = self.keep.astype(F32) + self.theirs.astype(F32)

    def send_last(self):
        high, low = self.left
        quarters = self.held.reshape(4, *self.held.shape[2:])
        place = (self.me // low) % 4
        self.keep = lax.dynamic_index_in_dim(quarters, place, 0, keepdims=False).astype(F32)
        self.aways = [
            lax.dynamic_index_in_dim(quarters, place ^ k, 0, keepdims=False).astype(BF16)
            for k in range(1, 4)
        ]
        self.parts = [swap(self.aways[k - 1], "dp", self.size, k * low) for k in range(1, 4)]

    def take_last(self):
        one, two, three = [part.astype(F32) for part in self.parts]
        self.held = (self.keep + one) + (two + three)


def sum_over(value, axis, size, bits):
    if len(bits) == 1:
        return value + swap(value, axis, size, bits[0])
    far, near = bits
    parts = together(*[swap(value, axis, size, bit) for bit in (near, far, far + near)])
    return (value + parts[0]) + (parts[1] + parts[2])


def tables(lengths, count):
    doc_ends = jnp.cumsum(lengths)
    places = jnp.arange(count, dtype=jnp.int32)
    after_end = places[:, None] >= doc_ends[None, :]
    begins = jnp.max(jnp.where(after_end, doc_ends[None, :], 0), axis=1)
    offset_f = (places - begins).astype(F32)
    frequency = jnp.exp(
        -(2.0 * jnp.arange(HALF_ROT, dtype=F32) / ROT_DIM) * math.log(10000.0)
    )
    angle = frequency[:, None] * offset_f[None, :]
    low_block = begins.reshape(count // QB, QB)[:, 0] // QB
    return begins[None, :], low_block, jnp.cos(angle), jnp.sin(angle)


def body(
    n_dp, n_row, tokens, ln_gain, ln_bias, w_query, w_key, w_value, w_out, w_up, w_down, doc_lengths, cotangent
):
    shard, width = tokens.shape
    total = shard * n_row
    own = width // n_row
    hid = w_up.shape[1]
    dp_me = lax.axis_index("dp")
    row_me = lax.axis_index("row").astype(jnp.int32)
    me = row_me.reshape(1)
    bits = bits_of(n_dp)
    to_core = partial(swap, axis="row", size=n_row, bit=1)
    to_chip = partial(swap, axis="row", size=n_row, bit=2)
    to_both = partial(swap, axis="row", size=n_row, bit=3)

    tok = [tokens, to_core(tokens), to_chip(tokens)]
    grad = [cotangent, to_core(cotangent)]
    up = Gather(w_up, n_dp, dp_me)
    down = Gather(w_down.T, n_dp, dp_me)
    orders = list(zip(bits, bits[-1:] + bits[:-1]))
    attn_shard = jnp.concatenate([w_query, w_key, w_value, w_out.T], axis=1)
    attn = Gather(attn_shard, n_dp, dp_me)
    for k, (first, second) in enumerate(orders):
        up.send(first)
        down.send(second)
        if k == 0:
            for bit in bits[:1:-1]:
                attn.send(bit)
                attn_ready = attn.theirs
                merge([attn])
        merge([up, down], (attn_ready, tok[2]) if k + 2 == len(orders) else ())
    grad.append(to_chip(cotangent))
    begin, low_block, cosine, sine = tables(doc_lengths[0], total)
    gain, bias = ln_gain[None, :], ln_bias[None, :]

    up_w, down_w = up.whole(), down.whole()
    quarter = attn.whole()
    quarters = [swap(quarter, "dp", n_dp, bit) for bit in (bits[1], bits[0], bits[0] + bits[1])]
    near_n, *near_mlp, near_dm, ffn_g = feed_forward(
        tok[:2], grad[:2], gain, bias, up_w, down_w, (), (quarter, cosine, sine, begin)
    )
    tok.append(to_core(after(tok[2], near_dm, *quarters)))
    grad[2] = after(grad[2], near_dm, *quarters)
    grad.append(to_core(grad[2]))
    wat, own_out = assemble((dp_me // bits[1]).astype(jnp.int32).reshape(1), [quarter, *quarters])
    far_n, *far_mlp, far_dm, ffn_g = feed_forward(
        tok[2:], grad[2:], gain, bias, up_w, down_w, (ffn_g,), (wat,)
    )
    ffn_wg = lax.psum_scatter(ffn_g, "dp", scatter_dimension=0, tiled=True)
    far_mlp_core = to_core(far_mlp[1])
    near_mlp_core = to_core(near_mlp[1])

    qkv, d_ctx = project(me, [near_n, far_n], grad, wat, cosine, sine)
    far_mlp_core = after(far_mlp_core, qkv)
    mlp_both = (far_mlp[0].astype(F32) + far_mlp_core.astype(F32)).astype(BF16)
    mlp_chip = to_chip(mlp_both)
    out_w = [own_out]
    out_w += [to_core(out_w[0]), to_chip(out_w[0]), to_both(out_w[0])]

    *ctx, dq, kv = attention(
        low_block, me, qkv, d_ctx, begin, cosine, sine, (mlp_both,)
    )

    ctxs = [ctx[0], to_core(ctx[1])]
    far_dn, far_dn_b, *sofar = finish(
        me, ctx[2:], dq, kv, tok[2:], grad[2:], far_n, far_dm, wat, 2, (), (mlp_chip, *out_w[1:])
    )
    theirs = to_core(far_dn_b)
    both = (far_dn.astype(F32) + theirs.astype(F32)).astype(BF16)
    away = jnp.concatenate([both, ctx[2], ctx[3]], axis=0)
    chip_got = to_chip(away)
    near_dn, near_dn_b, sums, attn_g = finish(
        me, ctx[:2], dq, kv, tok[:2], grad[:2], near_n, near_dm, wat, 0, sofar,
        (away, ffn_wg),
    )
    dn_core = to_core(near_dn_b)
    attn_sum = Scatter(attn_g, n_dp, dp_me)
    for bit in bits[:2:-1]:
        attn_sum.send(bit)
        attn_sum.take()
        sums = sum_over(sums, "dp", n_dp, [bit])
    attn_sum.send(bits[2])
    sums = sum_over(after(sums, attn_sum.away), "dp", n_dp, bits[:2])
    attn_sum.theirs = after(attn_sum.theirs, sums)
    attn_sum.take()
    attn_sum.send_last()
    sums = sum_over(after(sums, *attn_sum.aways), "dp", n_dp, bits[2:3])
    sums = sum_over(sums, "row", n_row, [2, 1])
    last_ctx = to_core(chip_got[shard + own :])
    mixed, input_grad = row_outputs(
        tokens,
        cotangent,
        gain,
        [near_dn, dn_core, chip_got],
        [near_mlp[0], near_mlp_core, mlp_chip],
        ctxs,
        chip_got,
        last_ctx,
        out_w,
        attn_sum.aways,
    )
    attn_sum.parts[0] = after(attn_sum.parts[0], input_grad)
    attn_sum.take_last()

    attn_wg, ffn_wg = attn_sum.held, ffn_wg.astype(F32)
    return (
        mixed,
        input_grad,
        sums[0],
        sums[1],
        attn_wg[:, :own],
        attn_wg[:, own : 2 * own],
        attn_wg[:, 2 * own : 3 * own],
        attn_wg[:, 3 * own :].T,
        ffn_wg[:, :hid],
        ffn_wg[:, hid:].T,
    )


def solution(mesh):
    in_specs = (
        P(("dp", "row"), None),
        P(),
        P(),
        P("dp", "row"),
        P("dp", "row"),
        P("dp", "row"),
        P("row", "dp"),
        P("dp", "row"),
        P("row", "dp"),
        P("dp", None),
        P(("dp", "row"), None),
    )
    out_specs = (
        P(("dp", "row"), None),
        P(("dp", "row"), None),
        P(),
        P(),
        P("dp", "row"),
        P("dp", "row"),
        P("dp", "row"),
        P("row", "dp"),
        P("dp", "row"),
        P("row", "dp"),
    )
    sizes = (mesh.shape["dp"], mesh.shape["row"])
    return jax.shard_map(
        partial(body, *sizes), mesh=mesh, in_specs=in_specs, out_specs=out_specs, check_vma=False
    )
```
